256 devices in a mesh: slab: 4 (over x), ranges: 64 (over y, z, core).
Axes of the slice: x: 4, y: 4, z: 8, core: 2. Of those that a mesh axis runs over, the one named last changes fastest.
Arguments:
- state: float32 [9, 1310720], P(None, ('slab', 'ranges'))
- keys: int32 [1310720], P(('slab', 'ranges')), may hold values from 0 to 524287, as said below
- halo_list: int32 [5120], P(('slab', 'ranges')), may hold values from 0 to 39, as said below
- neighbour_block_table: int32 [10240, 4], P(('slab', 'ranges')), may hold values from 0 to 59, as said below
- neighbour_block_count: int32 [10240], P(('slab', 'ranges')), may hold values from 1 to 4, as said below
Outputs:
- migrated: float32 [24, 2621440], P(None, ('slab', 'ranges'))
- step_size: float32 [], replicated
The draws below stay inside these ranges and needn't reach their ends.
Inputs may be any that keep to these rules, and one draw needn't show every extreme that they name: `keys`: key // 2048 of every particle lies among the 64 ranges of its own slab; from one device at most 160 particles go to one owner, and on every device some owner receives exactly 160. `halo_list`: the 20 entries of one device are distinct local block numbers. `neighbour_block_table`: entry 0 of a block's list is the block's own local number; the entries of one list are distinct. `neighbour_block_count`: every device has a block with 4 live entries.
All inputs are finite; a program needn't handle non-finite values.
Results may differ from the reference program's by a relative error of at most 0.0003.
Values sent between devices are 32-bit elements; how exact they have to be, the bound alone decides.
A program may use at most 64 MiB of HBM per device.

```python
from functools import partial
import jax
import jax.numpy as jnp
from jax import lax

FIELDS = 24
STATE_FIELDS = 9
BLOCK = 128
BLOCKS_DEV = 40
TILES = 4
KEY_SPAN = 2048
HALO = 10
CAP = 160
PARTICLES = 1310720
SLOTS = 2621440
BLOCK_COUNT = 10240
N_SLAB = 4
N_RANGES = 64


BOX_SIDE = 4.0


def draw_state(key, part):
    key = jax.random.fold_in(key, 11)
    key_list = jax.random.split(key, 5)
    count = PARTICLES
    position = jax.random.uniform(key_list[0], (3, count), jnp.float32, 0.0, BOX_SIDE)
    velocity = jax.random.normal(key_list[1], (3, count), jnp.float32)
    smooth = jnp.exp(jax.random.uniform(key_list[2], (1, count), jnp.float32, jnp.log(0.48), jnp.log(1.04)))
    mass = jnp.exp(jax.random.uniform(key_list[3], (1, count), jnp.float32, jnp.log(0.128), jnp.log(0.384)))
    energy = jnp.exp(jax.random.uniform(key_list[4], (1, count), jnp.float32, jnp.log(0.5), jnp.log(5.0)))
    return jnp.concatenate([position, velocity, smooth, mass, energy], axis=0).astype(jnp.float32)


def draw_keys(key, part):
    key = jax.random.fold_in(key, 23)
    device_count = N_SLAB * N_RANGES
    per_device = BLOCK * BLOCKS_DEV
    key_list = jax.random.split(key, 4)
    orders = jax.vmap(lambda sub: jax.random.permutation(sub, per_device))(jax.random.split(key_list[0], device_count))
    owner_rank = orders % N_RANGES
    hot_rank = jax.random.randint(key_list[1], (device_count, 1), 0, N_RANGES)
    cold_rank = (hot_rank + 1 + jax.random.randint(key_list[2], (device_count, 1), 0, N_RANGES - 1)) % N_RANGES
    owner_rank = jnp.where(owner_rank == cold_rank, hot_rank, owner_rank)
    slab_index = (jnp.arange(device_count) // N_RANGES)[:, None]
    lower = jax.random.randint(key_list[3], (device_count, per_device), 0, KEY_SPAN)
    return ((slab_index * N_RANGES + owner_rank) * KEY_SPAN + lower).reshape(-1).astype(jnp.int32)


def draw_halo_list(key, part):
    key = jax.random.fold_in(key, 31)
    device_count = N_SLAB * N_RANGES

    def one_device(sub):
        return jax.random.permutation(sub, BLOCKS_DEV)[:2 * HALO]
    return jax.vmap(one_device)(jax.random.split(key, device_count)).reshape(-1).astype(jnp.int32)


def draw_neighbour_block_table(key, part):
    key = jax.random.fold_in(key, 47)
    reach = BLOCKS_DEV + 2 * HALO
    homes = (jnp.arange(BLOCK_COUNT) % BLOCKS_DEV).astype(jnp.int32)

    def per_block(sub, home):
        others = jax.random.permutation(sub, reach - 1)[:TILES - 1].astype(jnp.int32)
        others = jnp.where(others >= home, others + 1, others)
        return jnp.concatenate([home[None], others])
    return jax.vmap(per_block)(jax.random.split(key, BLOCK_COUNT), homes).astype(jnp.int32)


def draw_neighbour_block_count(key, part):
    key = jax.random.fold_in(key, 59)
    first_key, second_key = jax.random.split(key)
    device_count = N_SLAB * N_RANGES
    totals = jax.random.randint(first_key, (device_count, BLOCKS_DEV), 1, TILES + 1)
    chosen = jax.random.randint(second_key, (device_count, 1), 0, BLOCKS_DEV)
    totals = jnp.where(jnp.arange(BLOCKS_DEV)[None, :] == chosen, TILES, totals)
    return totals.reshape(-1).astype(jnp.int32)


def setup_inputs(seed: int = 0) -> dict:
    key_of = jax.random.split(jax.random.key(seed), 6)
    return {
        "state": draw_state(jax.random.fold_in(key_of[5], 71), 0),
        "keys": draw_keys(jax.random.fold_in(key_of[5], 71), 0),
        "halo_list": draw_halo_list(jax.random.fold_in(key_of[5], 71), 0),
        "neighbour_block_table": draw_neighbour_block_table(jax.random.fold_in(key_of[5], 71), 0),
        "neighbour_block_count": draw_neighbour_block_count(jax.random.fold_in(key_of[5], 71), 0),
    }


GAMMA = 5.0 / 3.0
COURANT = 0.3
SMOOTH_ETA = 1.2
REGULAR = 0.02

def kernel(distance, smooth):
    scaled = distance / smooth
    profile = 0.25 * jnp.maximum(2.0 - scaled, 0.0) ** 3 - jnp.maximum(1.0 - scaled, 0.0) ** 3
    return profile / (jnp.pi * smooth ** 3)

def geometry(position_buffer, tile_index, position):
    nearby = position_buffer[:, tile_index]
    offset = nearby[:, :, None, :] - position[:, None, :, None]
    distance = jnp.sqrt(lax.optimization_barrier(jnp.sum(offset * offset, axis=0)))
    return (offset, distance)

def live_mask(tile_index, tile_total):
    return (jnp.arange(tile_index.shape[0]) < tile_total).astype(jnp.float32)[:, None, None]

def sym_apply(pair_coefficient, offset):
    grad_x = pair_coefficient[0] * offset[0] + pair_coefficient[1] * offset[1] + pair_coefficient[2] * offset[2]
    grad_y = pair_coefficient[1] * offset[0] + pair_coefficient[3] * offset[1] + pair_coefficient[4] * offset[2]
    grad_z = pair_coefficient[2] * offset[0] + pair_coefficient[4] * offset[1] + pair_coefficient[5] * offset[2]
    return (grad_x, grad_y, grad_z)

def density_pass(position_buffer, mass_space, position_local, smoothing_local, neighbour_block_table, neighbour_block_count):

    def per_block(block_members):
        tile_index, tile_total, position, smooth = block_members
        offset, distance = geometry(position_buffer, tile_index, position)
        weight = kernel(distance, smooth[None, :, None]) * live_mask(tile_index, tile_total)
        return lax.optimization_barrier(jnp.sum(weight * mass_space[tile_index][:, None, :], axis=(0, 2)))
    return lax.map(per_block, (neighbour_block_table, neighbour_block_count, jnp.moveaxis(position_local, 1, 0), smoothing_local))

def integral_gradient_sweep(position_buffer, volume_buffer, velocity_buffer, position_local, smoothing_local, velocity_local, neighbour_block_table, neighbour_block_count):

    def per_block(block_members):
        tile_index, tile_total, position, smooth, velocity = block_members
        offset, distance = geometry(position_buffer, tile_index, position)
        weight = kernel(distance, smooth[None, :, None]) * live_mask(tile_index, tile_total)
        weight = weight * volume_buffer[tile_index][:, None, :]
        moment = lax.optimization_barrier(jnp.sum(weight, axis=(0, 2)))
        tau_xx = lax.optimization_barrier(jnp.sum(weight * offset[0] * offset[0], axis=(0, 2)))
        tau_xy = lax.optimization_barrier(jnp.sum(weight * offset[0] * offset[1], axis=(0, 2)))
        tau_xz = lax.optimization_barrier(jnp.sum(weight * offset[0] * offset[2], axis=(0, 2)))
        tau_yy = lax.optimization_barrier(jnp.sum(weight * offset[1] * offset[1], axis=(0, 2)))
        tau_yz = lax.optimization_barrier(jnp.sum(weight * offset[1] * offset[2], axis=(0, 2)))
        tau_zz = lax.optimization_barrier(jnp.sum(weight * offset[2] * offset[2], axis=(0, 2)))
        diagonal = REGULAR * smooth * smooth * moment
        tau_xx = tau_xx + diagonal
        tau_yy = tau_yy + diagonal
        tau_zz = tau_zz + diagonal
        cof_xx = tau_yy * tau_zz - tau_yz * tau_yz
        cof_xy = tau_xz * tau_yz - tau_xy * tau_zz
        cof_xz = tau_xy * tau_yz - tau_xz * tau_yy
        cof_yy = tau_xx * tau_zz - tau_xz * tau_xz
        cof_yz = tau_xy * tau_xz - tau_xx * tau_yz
        cof_zz = tau_xx * tau_yy - tau_xy * tau_xy
        determinant = tau_xx * cof_xx + tau_xy * cof_xy + tau_xz * cof_xz
        pair_coefficient = jnp.stack([cof_xx, cof_xy, cof_xz, cof_yy, cof_yz, cof_zz]) / determinant
        gradient = sym_apply(pair_coefficient[:, None, :, None], offset)
        relative = velocity_buffer[:, tile_index][:, :, None, :] - velocity[:, None, :, None]
        flow = relative[0] * gradient[0] + relative[1] * gradient[1] + relative[2] * gradient[2]
        return (pair_coefficient, lax.optimization_barrier(jnp.sum(weight * flow, axis=(0, 2))))
    return lax.map(per_block, (neighbour_block_table, neighbour_block_count, jnp.moveaxis(position_local, 1, 0), smoothing_local, jnp.moveaxis(velocity_local, 1, 0)))

def momentum_pass(position_buffer, smooth_space, mass_space, velocity_buffer, density_buffer, coef_space, press_space, position_local, smoothing_local, velocity_local, coef_owned, factor_owned, neighbour_block_table, neighbour_block_count):
    factor_space = press_space / density_buffer ** 2

    def per_block(block_members):
        tile_index, tile_total, position, smooth, velocity, pair_coefficient, factor = block_members
        offset, distance = geometry(position_buffer, tile_index, position)
        live = live_mask(tile_index, tile_total)
        own_weight = kernel(distance, smooth[None, :, None]) * live
        near_weight = kernel(distance, smooth_space[tile_index][:, None, :]) * live
        own_grad = sym_apply(pair_coefficient[:, None, :, None], offset)
        near_grad = sym_apply(coef_space[:, tile_index][:, :, None, :], offset)
        near_mass = mass_space[tile_index][:, None, :]
        near_factor = factor_space[tile_index][:, None, :]
        own_factor = factor[None, :, None]
        accel = [-lax.optimization_barrier(jnp.sum(near_mass * (own_factor * own_grad[axis_id] * own_weight + near_factor * near_grad[axis_id] * near_weight), axis=(0, 2))) for axis_id in range(3)]
        relative = velocity[:, None, :, None] - velocity_buffer[:, tile_index][:, :, None, :]
        work = relative[0] * own_grad[0] + relative[1] * own_grad[1] + relative[2] * own_grad[2]
        heating = factor * lax.optimization_barrier(jnp.sum(near_mass * work * own_weight, axis=(0, 2)))
        return (jnp.stack(accel), heating)
    return lax.map(per_block, (neighbour_block_table, neighbour_block_count, jnp.moveaxis(position_local, 1, 0), smoothing_local, jnp.moveaxis(velocity_local, 1, 0), jnp.moveaxis(coef_owned, 1, 0), factor_owned))

def criterion(velocity, smooth, energy):
    speed = jnp.sqrt(lax.optimization_barrier(jnp.sum(velocity * velocity, axis=0)))
    return smooth / (jnp.sqrt(GAMMA * (GAMMA - 1.0) * energy) + speed)

def assemble(position, velocity, smooth, mass, energy, density, pair_coefficient, velocity_divergence, acceleration, heating, step_size):
    vel_new = velocity + step_size * acceleration
    pos_new = position + step_size * vel_new
    energy_new = energy + step_size * heating
    smooth_new = SMOOTH_ETA * jnp.cbrt(mass / density)
    pressure = (GAMMA - 1.0) * density * energy
    sound_speed = jnp.sqrt(GAMMA * (GAMMA - 1.0) * energy)
    return jnp.concatenate([pos_new, vel_new, smooth_new[None], mass[None], energy_new[None], density[None], pressure[None], sound_speed[None], pair_coefficient, acceleration, heating[None], energy[None], velocity_divergence[None]], axis=0)

def pack_slots(fields, key_row, ranges, capacity):
    owner_rank = key_row // KEY_SPAN % ranges
    onehot = (owner_rank[:, None] == jnp.arange(ranges)[None, :]).astype(jnp.int32)
    order_rank = lax.optimization_barrier(jnp.sum(jnp.cumsum(onehot, axis=0) * onehot, axis=1)) - 1
    slot_index = (owner_rank * capacity + order_rank).astype(jnp.int32)
    return jnp.zeros((fields.shape[0], ranges * capacity), fields.dtype).at[:, slot_index].set(fields)

def pick_blocks(fields, chosen):
    return fields[:, chosen]

def reference(state, keys, halo_list, neighbour_block_table, neighbour_block_count):
    device_count = N_SLAB * N_RANGES
    owned = jnp.moveaxis(state.reshape(STATE_FIELDS, device_count, BLOCKS_DEV, BLOCK), 1, 0)
    rim_lists = halo_list.reshape(device_count, 2 * HALO)
    tile_rows = neighbour_block_table.reshape(device_count, BLOCKS_DEV, TILES)
    tile_totals = neighbour_block_count.reshape(device_count, BLOCKS_DEV)

    def with_rims(fields):
        packed = jax.vmap(pick_blocks)(fields, rim_lists)
        from_prev = jnp.roll(packed[:, :, HALO:], 1, axis=0)
        from_next = jnp.roll(packed[:, :, :HALO], -1, axis=0)
        return jnp.concatenate([fields, from_prev, from_next], axis=2)
    position = owned[:, 0:3]
    velocity = owned[:, 3:6]
    smooth = owned[:, 6]
    mass = owned[:, 7]
    energy = owned[:, 8]
    first_space = with_rims(owned[:, 0:8])

    def device_density(block_members):
        border_buffer, position_shards, smoothing_shards, tile_shards, totals_shards = block_members
        return density_pass(border_buffer[0:3], border_buffer[7], position_shards, smoothing_shards, tile_shards, totals_shards)
    density = lax.map(device_density, (first_space, position, smooth, tile_rows, tile_totals))
    second_space = with_rims(density[:, None])

    def device_gradient(block_members):
        border_buffer, density_buffer, position_shards, smoothing_shards, velocity_shards, tile_shards, totals_shards = block_members
        return integral_gradient_sweep(border_buffer[0:3], border_buffer[7] / density_buffer[0], border_buffer[3:6], position_shards, smoothing_shards, velocity_shards, tile_shards, totals_shards)
    pair_coefficient, velocity_divergence = lax.map(device_gradient, (first_space, second_space, position, smooth, velocity, tile_rows, tile_totals))
    pair_coefficient = jnp.moveaxis(pair_coefficient, 2, 1)
    pressure = (GAMMA - 1.0) * density * energy
    third_space = with_rims(jnp.concatenate([pair_coefficient, pressure[:, None]], axis=1))

    def device_force(block_members):
        border_buffer, density_buffer, grad_space, position_shards, smoothing_shards, velocity_shards, coef_dev, factor_dev, tile_shards, totals_shards = block_members
        return momentum_pass(border_buffer[0:3], border_buffer[6], border_buffer[7], border_buffer[3:6], density_buffer[0], grad_space[0:6], grad_space[6], position_shards, smoothing_shards, velocity_shards, coef_dev, factor_dev, tile_shards, totals_shards)
    factor = pressure / density ** 2
    acceleration, heating = lax.map(device_force, (first_space, second_space, third_space, position, smooth, velocity, pair_coefficient, factor, tile_rows, tile_totals))
    acceleration = jnp.moveaxis(acceleration, 2, 1)
    step_size = COURANT * jnp.min(jax.vmap(criterion)(velocity, smooth, energy))
    fields = jax.vmap(assemble, in_axes=(0, 0, 0, 0, 0, 0, 0, 0, 0, 0, None))(position, velocity, smooth, mass, energy, density, pair_coefficient, velocity_divergence, acceleration, heating, step_size)
    fields = fields.reshape(device_count, FIELDS, BLOCKS_DEV * BLOCK)
    outgoing = jax.vmap(partial(pack_slots, ranges=N_RANGES, capacity=CAP))(fields, keys.reshape(device_count, BLOCKS_DEV * BLOCK))
    outgoing = outgoing.reshape(N_SLAB, N_RANGES, FIELDS, N_RANGES, CAP).transpose(0, 3, 2, 1, 4)
    outgoing = outgoing.reshape(device_count, FIELDS, N_RANGES * CAP)
    migrated = jnp.moveaxis(outgoing, 1, 0).reshape(FIELDS, SLOTS)
    return (migrated, step_size)
```

```python
import functools

import jax
import jax.numpy as jnp
from jax import lax
from jax.experimental import pallas as pl
from jax.experimental.pallas import tpu as pltpu
from jax.sharding import PartitionSpec as P

KEY_SPAN = 2048
GAMMA = 5.0 / 3.0
COURANT = 0.3
SMOOTH_ETA = 1.2
REGULAR = 0.02

LANES = 128
SUB = 8
MAIN = 128
REST = 32
TINY = 1e-30
FAR = 4.0
MESH = pl.DeviceIdType.MESH
VMEM = pl.BlockSpec(memory_space=pltpu.VMEM)
SMEM = pl.BlockSpec(memory_space=pltpu.SMEM)
GRANT = 52 * 1024 * 1024


def params(**more):
    return pltpu.CompilerParams(vmem_limit_bytes=GRANT, **more)


def curve_neighbours():
    slabs, ranges = lax.axis_size("slab"), lax.axis_size("ranges")
    me = lax.axis_index("slab") * ranges + lax.axis_index("ranges")
    after = lax.rem(me + 1, slabs * ranges)
    before = lax.rem(me + slabs * ranges - 1, slabs * ranges)
    return [(d // ranges, lax.rem(d, ranges)) for d in (before, after)]


def swap_halo(own_ref, halo_ref, packed, landed, send_sem, recv_sem, span):
    before, after = curve_neighbours()
    for i in range(2 * span):
        packed[i] = own_ref[halo_ref[i]]
    copies = []
    for side, target in ((0, before), (1, after)):
        copy = pltpu.make_async_remote_copy(
            src_ref=packed.at[pl.ds(side * span, span)],
            dst_ref=landed.at[pl.ds((1 - side) * span, span)],
            send_sem=send_sem.at[side],
            recv_sem=recv_sem.at[side],
            device_id=target,
            device_id_type=MESH,
        )
        copy.start()
        copies.append(copy)
    return copies


def greet(partners):
    barrier = pltpu.get_barrier_semaphore()
    for partner in partners:
        pl.semaphore_signal(barrier, inc=1, device_id=partner, device_id_type=MESH)
    pl.semaphore_wait(barrier, len(partners))


def halo_kernel(span, own_ref, halo_ref, out_ref, packed, landed, send_sem, recv_sem):
    greet(curve_neighbours())
    for copy in swap_halo(own_ref, halo_ref, packed, landed, send_sem, recv_sem, span):
        copy.wait()
    out_ref[...] = landed[...]


def halo_call(own, halo, number):
    span = halo.shape[0] // 2
    shape = (2 * span,) + own.shape[1:]
    return pl.pallas_call(
        functools.partial(halo_kernel, span),
        out_shape=jax.ShapeDtypeStruct(shape, own.dtype),
        in_specs=[VMEM, SMEM],
        out_specs=VMEM,
        scratch_shapes=[
            pltpu.VMEM(shape, own.dtype),
            pltpu.VMEM(shape, own.dtype),
            pltpu.SemaphoreType.DMA((2,)),
            pltpu.SemaphoreType.DMA((2,)),
        ],
        compiler_params=params(collective_id=number, has_side_effects=True),
    )(own, halo)


def groups():
    slabs, ranges = lax.axis_size("slab"), lax.axis_size("ranges")
    slab, rank = lax.axis_index("slab"), lax.axis_index("ranges")
    low = 8
    high = ranges // low
    r_high, r_low = rank // low, lax.rem(rank, low)
    return [
        [(slab, r_high * low + lax.rem(r_low + t, low)) for t in range(1, low)],
        [(slab, lax.rem(r_high + t, high) * low + r_low) for t in range(1, high)],
        [(lax.rem(slab + t, slabs), rank) for t in range(1, slabs)],
    ]


def first_kernel(
    span, own_ref, halo_ref, least_ref, out_ref, min_ref, packed, landed, send_sem, recv_sem, held, inbox, put_sem, got_sem
):
    stages = groups()
    greet(curve_neighbours() + [p for stage in stages for p in stage])
    copies = swap_halo(own_ref, halo_ref, packed, landed, send_sem, recv_sem, span)
    value = least_ref[...]
    slot = 0
    for n, stage in enumerate(stages):
        held[n] = value
        sent = []
        for partner in stage:
            copy = pltpu.make_async_remote_copy(
                src_ref=held.at[n],
                dst_ref=inbox.at[slot],
                send_sem=put_sem.at[slot],
                recv_sem=got_sem.at[slot],
                device_id=partner,
                device_id_type=MESH,
            )
            copy.start()
            sent.append((slot, copy))
            slot += 1
        for place, copy in sent:
            copy.wait()
            value = jnp.minimum(value, inbox[place])
    min_ref[...] = value
    for copy in copies:
        copy.wait()
    out_ref[...] = landed[...]


def first_call(own, halo, least):
    span = halo.shape[0] // 2
    shape = (2 * span,) + own.shape[1:]
    slabs, ranges = lax.axis_size("slab"), lax.axis_size("ranges")
    slots = 7 + (ranges // 8 - 1) + (slabs - 1)
    return pl.pallas_call(
        functools.partial(first_kernel, span),
        out_shape=(jax.ShapeDtypeStruct(shape, own.dtype), jax.ShapeDtypeStruct(least.shape, least.dtype)),
        in_specs=[VMEM, SMEM, VMEM],
        out_specs=(VMEM, VMEM),
        scratch_shapes=[
            pltpu.VMEM(shape, own.dtype),
            pltpu.VMEM(shape, own.dtype),
            pltpu.SemaphoreType.DMA((2,)),
            pltpu.SemaphoreType.DMA((2,)),
            pltpu.VMEM((3,) + least.shape, least.dtype),
            pltpu.VMEM((slots,) + least.shape, least.dtype),
            pltpu.SemaphoreType.DMA((slots,)),
            pltpu.SemaphoreType.DMA((slots,)),
        ],
        compiler_params=params(collective_id=1, has_side_effects=True),
    )(own, halo, least)


def spread(rows, start, wide_ref, base, fields):
    total = len(fields)
    x = jnp.concatenate(rows, axis=1)
    high = x.astype(jnp.bfloat16).astype(jnp.float32)
    middle = (x - high).astype(jnp.bfloat16).astype(jnp.float32)
    parts = jnp.concatenate([high, middle, x - high - middle], axis=0).astype(jnp.bfloat16)
    kind = lax.rem(lax.broadcasted_iota(jnp.int32, (3 * SUB, LANES), 0), SUB)
    picks = [(kind == f).astype(jnp.float32).astype(jnp.bfloat16) for f in fields]
    length = x.shape[1]
    at = pl.ds(pl.multiple_of(start * LANES, LANES), length)
    for n in range(0, total, 2):
        pick = jnp.concatenate(picks[n : n + 2], axis=1)
        out = lax.dot_general(parts, pick, (((0,), (0,)), ((), ())), preferred_element_type=jnp.float32)
        for m in range(min(2, total - n)):
            wide_ref[base + n + m, at, :] = out[:, m * LANES : (m + 1) * LANES]


def spread_all(make, count, first, wide_ref, base, fields, group=10):
    def turn(g, carry):
        spread([make(g * group + i) for i in range(group)], first + g * group, wide_ref, base, fields)
        return carry

    lax.fori_loop(0, count // group, turn, 0)


def profile(square):
    near = jnp.minimum(square, FAR)
    ratio = near * lax.rsqrt(jnp.maximum(near, TINY))
    outer = jnp.maximum(2.0 - ratio, 0.0)
    inner = jnp.maximum(outer - 1.0, 0.0)
    return outer * outer * (0.25 * outer) - inner * inner * inner


def full(row):
    return jnp.broadcast_to(row, (SUB, LANES))


def shear(w, u):
    return (
        u[0] * w[0],
        u[0] * w[1] + u[1] * w[0],
        u[0] * w[2] + u[2] * w[0],
        u[1] * w[1],
        u[1] * w[2] + u[2] * w[1],
        u[2] * w[2],
    )


def sweep(table, count, blocks, width, load, prepare, pair, sums_ref):
    tiles = table.shape[0] // blocks

    def block(b, carry):
        here = prepare(b)

        def tile(k, sums):
            start = table[b * tiles + k] * LANES
            for s in range(LANES // SUB):
                cols = load(pl.ds(pl.multiple_of(start + s * SUB, SUB), SUB))
                sums = pair(cols, here, sums)
            return sums

        zero = jnp.zeros((SUB, LANES), jnp.float32)
        sums = lax.fori_loop(0, count[b], tile, (zero,) * width)
        for f in range(width):
            sums_ref[f, pl.ds(b, 1), :] = jnp.sum(sums[f], axis=0, keepdims=True)
        return carry

    lax.fori_loop(0, blocks, block, 0)


def add(sums, terms):
    return tuple(s + t for s, t in zip(sums, terms))


def density_kernel(table, count, own_ref, halo_ref, smooth_ref, out_ref, wide_ref):
    blocks = own_ref.shape[0]
    fields = (0, 1, 2, 3, 4, 5, 7)
    spread_all(lambda b: own_ref[b], blocks, 0, wide_ref, 0, fields)
    spread_all(lambda b: halo_ref[b], halo_ref.shape[0], blocks, wide_ref, 0, fields)

    def prepare(b):
        h = own_ref[b, 6:7, :]
        return [full(own_ref[b, f : f + 1, :]) for f in range(6)] + [full(1.0 / (h * h))]

    def load(at):
        return [wide_ref[n, at, :] for n in range(7)]

    def pair(c, here, sums):
        d = [c[a] - here[a] for a in range(3)]
        square = d[0] * d[0] + d[1] * d[1] + d[2] * d[2]
        w = profile(square * here[6]) * c[6]
        wd = [w * d[a] for a in range(3)]
        u = [c[3 + a] - here[3 + a] for a in range(3)]
        return add(sums, (w, *wd, *shear(wd, u)))

    sweep(table, count, blocks, 10, load, prepare, pair, out_ref)
    h = smooth_ref[...]
    norm = 1.0 / (jnp.pi * h * h * h)
    for f in range(10):
        out_ref[f] = out_ref[f] * norm


def density_call(table, count, own, halo, smooth):
    blocks = own.shape[0]
    space = (blocks + halo.shape[0]) * LANES
    return pl.pallas_call(
        density_kernel,
        out_shape=jax.ShapeDtypeStruct((10, blocks, LANES), jnp.float32),
        in_specs=[SMEM, SMEM, VMEM, VMEM, VMEM],
        out_specs=VMEM,
        scratch_shapes=[pltpu.VMEM((7, space, LANES), jnp.float32)],
        compiler_params=params(),
    )(table, count, own, halo, smooth)


def gradient_kernel(
    table,
    count,
    own_ref,
    halo_ref,
    halo_density_ref,
    smooth_ref,
    mass_ref,
    energy_ref,
    first_ref,
    coef_ref,
    near_ref,
    wide_ref,
    sums_ref,
):
    blocks = own_ref.shape[0]
    fields = (0, 1, 2, 3, 4, 5, 7)

    def with_volume(rows, density):
        return jnp.concatenate([rows[0:7], rows[7:8] / density], axis=0)

    spread_all(lambda b: with_volume(own_ref[b], first_ref[0, pl.ds(b, 1), :]), blocks, 0, wide_ref, 0, fields)
    spread_all(
        lambda b: with_volume(halo_ref[b], halo_density_ref[pl.ds(b, 1), :]), halo_ref.shape[0], blocks, wide_ref, 0, fields
    )

    def prepare(b):
        h = own_ref[b, 6:7, :]
        return [full(own_ref[b, f : f + 1, :]) for f in range(6)] + [full(1.0 / (h * h))]

    def load(at):
        return [wide_ref[n, at, :] for n in range(7)]

    def pair(c, here, sums):
        d = [c[a] - here[a] for a in range(3)]
        square = d[0] * d[0] + d[1] * d[1] + d[2] * d[2]
        w = profile(square * here[6]) * c[6]
        wd = [w * d[a] for a in range(3)]
        u = [c[3 + a] - here[3 + a] for a in range(3)]
        tau = (wd[0] * d[0], wd[0] * d[1], wd[0] * d[2], wd[1] * d[1], wd[1] * d[2], wd[2] * d[2])
        return add(sums, (w, *tau, *shear(wd, u)))

    sweep(table, count, blocks, 13, load, prepare, pair, sums_ref)
    h = smooth_ref[...]
    norm = 1.0 / (jnp.pi * h * h * h)
    s = [sums_ref[f] * norm for f in range(13)]
    diagonal = REGULAR * h * h * s[0]
    xx, xy, xz, yy, yz, zz = s[1] + diagonal, s[2], s[3], s[4] + diagonal, s[5], s[6] + diagonal
    cof = (
        yy * zz - yz * yz,
        xz * yz - xy * zz,
        xy * yz - xz * yy,
        xx * zz - xz * xz,
        xy * xz - xx * yz,
        xx * yy - xy * xy,
    )
    determinant = xx * cof[0] + xy * cof[1] + xz * cof[2]
    coef = [c / determinant for c in cof]
    divergence = sum(c * t for c, t in zip(coef, s[7:13]))
    density = first_ref[0]
    factor = (GAMMA - 1.0) * density * energy_ref[...] / (density * density)
    heating = -factor * sum(coef[n] * first_ref[4 + n] for n in range(6))
    pull = [first_ref[1 + a] for a in range(3)]
    own_part = [
        factor * (coef[0] * pull[0] + coef[1] * pull[1] + coef[2] * pull[2]),
        factor * (coef[1] * pull[0] + coef[3] * pull[1] + coef[4] * pull[2]),
        factor * (coef[2] * pull[0] + coef[4] * pull[1] + coef[5] * pull[2]),
    ]
    for n, value in enumerate([*coef, divergence, *own_part, heating]):
        coef_ref[n] = value
    scale = mass_ref[...] * factor * norm
    inverse = 1.0 / (h * h)
    for n in range(6):
        sums_ref[n] = coef[n] * scale
    sums_ref[6] = inverse
    sums_ref[7] = inverse

    def regroup(b, carry):
        near_ref[b] = jnp.concatenate([sums_ref[n, pl.ds(b, 1), :] for n in range(8)], axis=0)
        return carry

    lax.fori_loop(0, blocks, regroup, 0)


def gradient_call(table, count, own, halo, halo_density, smooth, mass, energy, first):
    blocks = own.shape[0]
    space = (blocks + halo.shape[0]) * LANES
    return pl.pallas_call(
        gradient_kernel,
        out_shape=(
            jax.ShapeDtypeStruct((11, blocks, LANES), jnp.float32),
            jax.ShapeDtypeStruct((blocks, SUB, LANES), jnp.float32),
        ),
        in_specs=[SMEM, SMEM] + [VMEM] * 7,
        out_specs=(VMEM, VMEM),
        scratch_shapes=[
            pltpu.VMEM((7, space, LANES), jnp.float32),
            pltpu.VMEM((13, blocks, LANES), jnp.float32),
        ],
        compiler_params=params(),
    )(table, count, own, halo, halo_density, smooth, mass, energy, first)


def force_kernel(table, count, own_ref, halo_ref, near_ref, halo_near_ref, out_ref, wide_ref):
    blocks = own_ref.shape[0]
    halos = halo_ref.shape[0]
    spread_all(lambda b: own_ref[b], blocks, 0, wide_ref, 0, (0, 1, 2))
    spread_all(lambda b: halo_ref[b], halos, blocks, wide_ref, 0, (0, 1, 2))
    spread_all(lambda b: near_ref[b], blocks, 0, wide_ref, 3, tuple(range(7)))
    spread_all(lambda b: halo_near_ref[b], halos, blocks, wide_ref, 3, tuple(range(7)))

    def prepare(b):
        return [full(own_ref[b, f : f + 1, :]) for f in range(3)]

    def load(at):
        return [wide_ref[n, at, :] for n in range(10)]

    def pair(c, here, sums):
        d = [c[a] - here[a] for a in range(3)]
        square = d[0] * d[0] + d[1] * d[1] + d[2] * d[2]
        w = profile(square * c[9])
        x, y, z = (w * d[a] for a in range(3))
        return (
            sums[0] + c[3] * x + c[4] * y + c[5] * z,
            sums[1] + c[4] * x + c[6] * y + c[7] * z,
            sums[2] + c[5] * x + c[7] * y + c[8] * z,
        )

    sweep(table, count, blocks, 3, load, prepare, pair, out_ref)


def force_call(table, count, own, halo, near, halo_near):
    blocks = own.shape[0]
    space = (blocks + halo.shape[0]) * LANES
    return pl.pallas_call(
        force_kernel,
        out_shape=jax.ShapeDtypeStruct((3, blocks, LANES), jnp.float32),
        in_specs=[SMEM, SMEM] + [VMEM] * 4,
        out_specs=VMEM,
        scratch_shapes=[pltpu.VMEM((10, space, LANES), jnp.float32)],
        compiler_params=params(),
    )(table, count, own, halo, near, halo_near)


def pack_kernel(place_ref, fields_ref, out_ref, slots_ref, rows_ref):
    count, blocks = fields_ref.shape[0], fields_ref.shape[1]
    owners = out_ref.shape[0]
    parts = count // SUB

    def clear(i, carry):
        slots_ref[pl.ds(pl.multiple_of(i * 128, 128), 128), :] = jnp.zeros((128, LANES), jnp.float32)
        return carry

    lax.fori_loop(0, slots_ref.shape[0] // 128, clear, 0)

    def block(b, carry):
        together = jnp.concatenate([fields_ref[f, pl.ds(b, 1), :] for f in range(count)], axis=0)
        rows_ref[:, 0:count] = jnp.transpose(together)
        for i in range(LANES):
            slots_ref[pl.ds(place_ref[b * LANES + i], 1), :] = rows_ref[i : i + 1, :]
        return carry

    lax.fori_loop(0, blocks, block, 0)

    def main(owner, carry):
        rows = slots_ref[pl.ds(pl.multiple_of(owner * MAIN, MAIN), MAIN), 0:count]
        out_ref[owner, 0:count, :] = jnp.transpose(rows)
        return carry

    lax.fori_loop(0, owners, main, 0)
    lane = lax.broadcasted_iota(jnp.int32, (SUB, LANES), 1) // REST

    def rest(g, carry):
        at = pl.multiple_of(owners * MAIN + g * LANES, LANES)
        turned = jnp.transpose(slots_ref[pl.ds(at, LANES), 0:count])
        for i in range(LANES // REST):
            mixed = jnp.zeros((SUB, LANES), jnp.float32)
            for v in range(parts):
                piece = turned[v * SUB : (v + 1) * SUB, :]
                shift = (v - i) * REST % LANES
                if shift:
                    piece = pltpu.roll(piece, shift, 1)
                mixed = jnp.where(lane == v, piece, mixed)
            out_ref[g * (LANES // REST) + i, count : count + SUB, :] = mixed
        return carry

    lax.fori_loop(0, owners * REST // LANES, rest, 0)


def pack_call(place, fields, owners):
    count, blocks = fields.shape[:2]
    return pl.pallas_call(
        pack_kernel,
        out_shape=jax.ShapeDtypeStruct((owners, count + SUB, LANES), jnp.float32),
        in_specs=[SMEM, VMEM],
        out_specs=VMEM,
        scratch_shapes=[
            pltpu.VMEM((owners * (MAIN + REST), LANES), jnp.float32),
            pltpu.VMEM((LANES, LANES), jnp.float32),
        ],
        compiler_params=params(),
    )(place, fields)


def unpack_kernel(in_ref, out_ref):
    sources = in_ref.shape[0]
    count = out_ref.shape[0]
    parts = count // SUB
    lane = lax.broadcasted_iota(jnp.int32, (SUB, LANES), 1)

    def turn(g, carry):
        for v in range(parts):
            columns = [None] * 5
            for i in range(4):
                q = g * 4 + i
                first = in_ref[q, v * SUB : (v + 1) * SUB, :]
                last = in_ref[q, count : count + SUB, :]
                start = i * (MAIN + REST)
                c, off = start // LANES, start % LANES
                moved = pltpu.roll(first, off, 1) if off else first
                columns[c] = moved if columns[c] is None else jnp.where(lane < off, columns[c], moved)
                if off:
                    columns[c + 1] = moved
                c, off = (start + MAIN) // LANES, (start + MAIN) % LANES
                shift = (off - v * REST) % LANES
                moved = pltpu.roll(last, shift, 1) if shift else last
                columns[c] = moved if columns[c] is None else jnp.where(lane < off, columns[c], moved)
            for c in range(5):
                at = pl.multiple_of(g * 5 * LANES + c * LANES, LANES)
                out_ref[v * SUB : (v + 1) * SUB, pl.ds(at, LANES)] = columns[c]
        return carry

    lax.fori_loop(0, sources // 4, turn, 0)


def unpack_call(received, count):
    sources = received.shape[0]
    return pl.pallas_call(
        unpack_kernel,
        out_shape=jax.ShapeDtypeStruct((count, sources * (MAIN + REST)), jnp.float32),
        in_specs=[VMEM],
        out_specs=VMEM,
        compiler_params=params(),
    )(received)


def slot_rows(keys, owners):
    owner = lax.rem(keys // KEY_SPAN, owners)
    blocks = owner.shape[0]
    onehot = (owner[:, None, :] == jnp.arange(owners)[None, :, None]).astype(jnp.bfloat16)
    before = (jnp.arange(LANES)[:, None] < jnp.arange(LANES)[None, :]).astype(jnp.bfloat16)
    inside = jnp.einsum("bok,kl->bol", onehot, before, preferred_element_type=jnp.float32)
    totals = jnp.sum(onehot.astype(jnp.float32), axis=2)
    earlier = (jnp.arange(blocks)[:, None] > jnp.arange(blocks)[None, :]).astype(jnp.float32)
    ahead = jnp.dot(earlier, totals, precision=lax.Precision.HIGHEST)
    rank = jnp.sum(onehot.astype(jnp.float32) * (inside + ahead[:, :, None]), axis=1).astype(jnp.int32)
    return jnp.where(rank < MAIN, owner * MAIN + rank, owners * MAIN + owner * REST + rank - MAIN)


def per_device(state, keys, halo_list, neighbour_block_table, neighbour_block_count):
    blocks = neighbour_block_table.shape[0]
    owners = lax.axis_size("ranges")
    table = neighbour_block_table.reshape(-1)
    count = neighbour_block_count
    rows = state.reshape(state.shape[0], blocks, LANES)
    position, velocity, smooth, mass, energy = rows[0:3], rows[3:6], rows[6], rows[7], rows[8]
    own = jnp.transpose(rows[0:8], (1, 0, 2))
    speed = jnp.sqrt(jnp.sum(velocity * velocity, axis=0))
    sound = jnp.sqrt(GAMMA * (GAMMA - 1.0) * energy)
    least = jnp.full((SUB, LANES), jnp.min(smooth / (sound + speed)), jnp.float32)
    place = slot_rows(keys.reshape(blocks, LANES), owners).reshape(-1)

    halo, smallest = first_call(own, halo_list, least)
    step_size = COURANT * smallest[0, 0]
    first = density_call(table, count, own, halo, smooth)
    density = first[0]
    halo_density = halo_call(density[:, None, :], halo_list, 2)[:, 0, :]
    coef, near = gradient_call(table, count, own, halo, halo_density, smooth, mass, energy, first)
    halo_near = halo_call(near, halo_list, 3)
    pull = force_call(table, count, own, halo, near, halo_near)

    acceleration = -(coef[7:10] + pull)
    heating = coef[10]
    vel_new = velocity + step_size * acceleration
    fields = jnp.concatenate(
        [
            position + step_size * vel_new,
            vel_new,
            (SMOOTH_ETA * jnp.cbrt(mass / density))[None],
            mass[None],
            (energy + step_size * heating)[None],
            density[None],
            ((GAMMA - 1.0) * density * energy)[None],
            sound[None],
            coef[0:6],
            acceleration,
            heating[None],
            energy[None],
            coef[6:7],
        ],
        axis=0,
    )
    packed = pack_call(place, fields, owners)
    received = lax.all_to_all(packed, "ranges", split_axis=0, concat_axis=0, tiled=True)
    return (unpack_call(received, fields.shape[0]), step_size)


def solution(mesh):
    both = ("slab", "ranges")
    return jax.shard_map(
        per_device,
        mesh=mesh,
        in_specs=(P(None, both), P(both), P(both), P(both, None), P(both)),
        out_specs=(P(None, both), P()),
        check_vma=False,
    )
```

```python
import functools

import jax
import jax.numpy as jnp
from jax import lax
from jax.experimental import pallas as pl
from jax.experimental.pallas import tpu as pltpu
from jax.sharding import PartitionSpec as P

KEY_SPAN = 2048
GAMMA = 5.0 / 3.0
COURANT = 0.3
SMOOTH_ETA = 1.2
REGULAR = 0.02

LANES = 128
SUB = 8
MAIN = 128
REST = 32
TINY = 1e-30
FAR = 4.0
MESH = pl.DeviceIdType.MESH
VMEM = pl.BlockSpec(memory_space=pltpu.VMEM)
SMEM = pl.BlockSpec(memory_space=pltpu.SMEM)
GRANT = 52 * 1024 * 1024


def params(**more):
    return pltpu.CompilerParams(vmem_limit_bytes=GRANT, **more)


def curve_neighbours():
    slabs, ranges = lax.axis_size("slab"), lax.axis_size("ranges")
    me = lax.axis_index("slab") * ranges + lax.axis_index("ranges")
    after = lax.rem(me + 1, slabs * ranges)
    before = lax.rem(me + slabs * ranges - 1, slabs * ranges)
    return [(d // ranges, lax.rem(d, ranges)) for d in (before, after)]


def swap_halo(own_ref, halo_ref, packed, landed, send_sem, recv_sem, span):
    before, after = curve_neighbours()
    for i in range(2 * span):
        packed[i] = own_ref[halo_ref[i]]
    copies = []
    for side, target in ((0, before), (1, after)):
        copy = pltpu.make_async_remote_copy(
            src_ref=packed.at[pl.ds(side * span, span)],
            dst_ref=landed.at[pl.ds((1 - side) * span, span)],
            send_sem=send_sem.at[side],
            recv_sem=recv_sem.at[side],
            device_id=target,
            device_id_type=MESH,
        )
        copy.start()
        copies.append(copy)
    return copies


def greet(partners):
    barrier = pltpu.get_barrier_semaphore()
    for partner in partners:
        pl.semaphore_signal(barrier, inc=1, device_id=partner, device_id_type=MESH)
    pl.semaphore_wait(barrier, len(partners))


def stage_partners(stage):
    slabs, ranges = lax.axis_size("slab"), lax.axis_size("ranges")
    slab, rank = lax.axis_index("slab"), lax.axis_index("ranges")
    low = 8
    high = ranges // low
    r_high, r_low = rank // low, lax.rem(rank, low)
    if stage == 0:
        return [(slab, r_high * low + lax.rem(r_low + t, low)) for t in range(1, low)]
    if stage == 1:
        return [(slab, lax.rem(r_high + t, high) * low + r_low) for t in range(1, high)]
    return [(lax.rem(slab + t, slabs), rank) for t in range(1, slabs)]


def exchange_kernel(
    span, stage, own_ref, halo_ref, least_ref, out_ref, min_ref, packed, landed, send_sem, recv_sem, inbox, put_sem, got_sem
):
    partners = stage_partners(stage)
    greet(curve_neighbours() + partners)
    copies = swap_halo(own_ref, halo_ref, packed, landed, send_sem, recv_sem, span)
    small = []
    for slot, partner in enumerate(partners):
        copy = pltpu.make_async_remote_copy(
            src_ref=least_ref,
            dst_ref=inbox.at[slot],
            send_sem=put_sem.at[slot],
            recv_sem=got_sem.at[slot],
            device_id=partner,
            device_id_type=MESH,
        )
        copy.start()
        small.append(copy)
    for copy in copies:
        copy.wait()
    out_ref[...] = landed[...]
    value = least_ref[...]
    for slot, copy in enumerate(small):
        copy.wait()
        value = jnp.minimum(value, inbox[slot])
    min_ref[...] = value


def exchange_call(own, halo, least, stage):
    span = halo.shape[0] // 2
    shape = (2 * span,) + own.shape[1:]
    slabs, ranges = lax.axis_size("slab"), lax.axis_size("ranges")
    slots = (7, ranges // 8 - 1, slabs - 1)[stage]
    return pl.pallas_call(
        functools.partial(exchange_kernel, span, stage),
        out_shape=(jax.ShapeDtypeStruct(shape, own.dtype), jax.ShapeDtypeStruct(least.shape, least.dtype)),
        in_specs=[VMEM, SMEM, VMEM],
        out_specs=(VMEM, VMEM),
        scratch_shapes=[
            pltpu.VMEM(shape, own.dtype),
            pltpu.VMEM(shape, own.dtype),
            pltpu.SemaphoreType.DMA((2,)),
            pltpu.SemaphoreType.DMA((2,)),
            pltpu.VMEM((slots,) + least.shape, least.dtype),
            pltpu.SemaphoreType.DMA((slots,)),
            pltpu.SemaphoreType.DMA((slots,)),
        ],
        compiler_params=params(collective_id=1 + stage, has_side_effects=True),
    )(own, halo, least)


def spread(rows, start, wide_ref, base, fields):
    total = len(fields)
    x = jnp.concatenate(rows, axis=1)
    high = x.astype(jnp.bfloat16).astype(jnp.float32)
    middle = (x - high).astype(jnp.bfloat16).astype(jnp.float32)
    parts = jnp.concatenate([high, middle, x - high - middle], axis=0).astype(jnp.bfloat16)
    kind = lax.rem(lax.broadcasted_iota(jnp.int32, (3 * SUB, LANES), 0), SUB)
    picks = [(kind == f).astype(jnp.float32).astype(jnp.bfloat16) for f in fields]
    length = x.shape[1]
    at = pl.ds(pl.multiple_of(start * LANES, LANES), length)
    for n in range(0, total, 2):
        pick = jnp.concatenate(picks[n : n + 2], axis=1)
        out = lax.dot_general(parts, pick, (((0,), (0,)), ((), ())), preferred_element_type=jnp.float32)
        for m in range(min(2, total - n)):
            wide_ref[base + n + m, at, :] = out[:, m * LANES : (m + 1) * LANES]


def spread_all(make, count, first, wide_ref, base, fields, group=10):
    def turn(g, carry):
        spread([make(g * group + i) for i in range(group)], first + g * group, wide_ref, base, fields)
        return carry

    lax.fori_loop(0, count // group, turn, 0)


def profile(square):
    near = jnp.minimum(square, FAR)
    ratio = near * lax.rsqrt(jnp.maximum(near, TINY))
    outer = jnp.maximum(2.0 - ratio, 0.0)
    inner = jnp.maximum(outer - 1.0, 0.0)
    return outer * outer * (0.25 * outer) - inner * inner * inner


def full(row):
    return jnp.broadcast_to(row, (SUB, LANES))


def shear(w, u):
    return (
        u[0] * w[0],
        u[0] * w[1] + u[1] * w[0],
        u[0] * w[2] + u[2] * w[0],
        u[1] * w[1],
        u[1] * w[2] + u[2] * w[1],
        u[2] * w[2],
    )


def sweep(table, count, blocks, width, load, prepare, pair, sums_ref):
    tiles = table.shape[0] // blocks

    def block(b, carry):
        here = prepare(b)

        def tile(k, sums):
            start = table[b * tiles + k] * LANES
            for s in range(LANES // SUB):
                cols = load(pl.ds(pl.multiple_of(start + s * SUB, SUB), SUB))
                sums = pair(cols, here, sums)
            return sums

        zero = jnp.zeros((SUB, LANES), jnp.float32)
        sums = lax.fori_loop(0, count[b], tile, (zero,) * width)
        for f in range(width):
            sums_ref[f, pl.ds(b, 1), :] = jnp.sum(sums[f], axis=0, keepdims=True)
        return carry

    lax.fori_loop(0, blocks, block, 0)


def add(sums, terms):
    return tuple(s + t for s, t in zip(sums, terms))


def density_kernel(table, count, own_ref, halo_ref, smooth_ref, out_ref, wide_ref):
    blocks = own_ref.shape[0]
    fields = (0, 1, 2, 3, 4, 5, 7)
    spread_all(lambda b: own_ref[b], blocks, 0, wide_ref, 0, fields)
    spread_all(lambda b: halo_ref[b], halo_ref.shape[0], blocks, wide_ref, 0, fields)

    def prepare(b):
        h = own_ref[b, 6:7, :]
        return [full(own_ref[b, f : f + 1, :]) for f in range(6)] + [full(1.0 / (h * h))]

    def load(at):
        return [wide_ref[n, at, :] for n in range(7)]

    def pair(c, here, sums):
        d = [c[a] - here[a] for a in range(3)]
        square = d[0] * d[0] + d[1] * d[1] + d[2] * d[2]
        w = profile(square * here[6]) * c[6]
        wd = [w * d[a] for a in range(3)]
        u = [c[3 + a] - here[3 + a] for a in range(3)]
        return add(sums, (w, *wd, *shear(wd, u)))

    sweep(table, count, blocks, 10, load, prepare, pair, out_ref)
    h = smooth_ref[...]
    norm = 1.0 / (jnp.pi * h * h * h)
    for f in range(10):
        out_ref[f] = out_ref[f] * norm


def density_call(table, count, own, halo, smooth):
    blocks = own.shape[0]
    space = (blocks + halo.shape[0]) * LANES
    return pl.pallas_call(
        density_kernel,
        out_shape=jax.ShapeDtypeStruct((10, blocks, LANES), jnp.float32),
        in_specs=[SMEM, SMEM, VMEM, VMEM, VMEM],
        out_specs=VMEM,
        scratch_shapes=[pltpu.VMEM((7, space, LANES), jnp.float32)],
        compiler_params=params(),
    )(table, count, own, halo, smooth)


def gradient_kernel(
    table,
    count,
    own_ref,
    halo_ref,
    halo_density_ref,
    smooth_ref,
    mass_ref,
    energy_ref,
    first_ref,
    coef_ref,
    near_ref,
    wide_ref,
    sums_ref,
):
    blocks = own_ref.shape[0]
    fields = (0, 1, 2, 3, 4, 5, 7)

    def with_volume(rows, density):
        return jnp.concatenate([rows[0:7], rows[7:8] / density], axis=0)

    spread_all(lambda b: with_volume(own_ref[b], first_ref[0, pl.ds(b, 1), :]), blocks, 0, wide_ref, 0, fields)
    spread_all(
        lambda b: with_volume(halo_ref[b], halo_density_ref[pl.ds(b, 1), :]), halo_ref.shape[0], blocks, wide_ref, 0, fields
    )

    def prepare(b):
        h = own_ref[b, 6:7, :]
        return [full(own_ref[b, f : f + 1, :]) for f in range(6)] + [full(1.0 / (h * h))]

    def load(at):
        return [wide_ref[n, at, :] for n in range(7)]

    def pair(c, here, sums):
        d = [c[a] - here[a] for a in range(3)]
        square = d[0] * d[0] + d[1] * d[1] + d[2] * d[2]
        w = profile(square * here[6]) * c[6]
        wd = [w * d[a] for a in range(3)]
        u = [c[3 + a] - here[3 + a] for a in range(3)]
        tau = (wd[0] * d[0], wd[0] * d[1], wd[0] * d[2], wd[1] * d[1], wd[1] * d[2], wd[2] * d[2])
        return add(sums, (w, *tau, *shear(wd, u)))

    sweep(table, count, blocks, 13, load, prepare, pair, sums_ref)
    h = smooth_ref[...]
    norm = 1.0 / (jnp.pi * h * h * h)
    s = [sums_ref[f] * norm for f in range(13)]
    diagonal = REGULAR * h * h * s[0]
    xx, xy, xz, yy, yz, zz = s[1] + diagonal, s[2], s[3], s[4] + diagonal, s[5], s[6] + diagonal
    cof = (
        yy * zz - yz * yz,
        xz * yz - xy * zz,
        xy * yz - xz * yy,
        xx * zz - xz * xz,
        xy * xz - xx * yz,
        xx * yy - xy * xy,
    )
    determinant = xx * cof[0] + xy * cof[1] + xz * cof[2]
    coef = [c / determinant for c in cof]
    divergence = sum(c * t for c, t in zip(coef, s[7:13]))
    density = first_ref[0]
    factor = (GAMMA - 1.0) * density * energy_ref[...] / (density * density)
    heating = -factor * sum(coef[n] * first_ref[4 + n] for n in range(6))
    pull = [first_ref[1 + a] for a in range(3)]
    own_part = [
        factor * (coef[0] * pull[0] + coef[1] * pull[1] + coef[2] * pull[2]),
        factor * (coef[1] * pull[0] + coef[3] * pull[1] + coef[4] * pull[2]),
        factor * (coef[2] * pull[0] + coef[4] * pull[1] + coef[5] * pull[2]),
    ]
    for n, value in enumerate([*coef, divergence, *own_part, heating]):
        coef_ref[n] = value
    scale = mass_ref[...] * factor * norm
    inverse = 1.0 / (h * h)
    for n in range(6):
        sums_ref[n] = coef[n] * scale
    sums_ref[6] = inverse
    sums_ref[7] = inverse

    def regroup(b, carry):
        near_ref[b] = jnp.concatenate([sums_ref[n, pl.ds(b, 1), :] for n in range(8)], axis=0)
        return carry

    lax.fori_loop(0, blocks, regroup, 0)


def gradient_call(table, count, own, halo, halo_density, smooth, mass, energy, first):
    blocks = own.shape[0]
    space = (blocks + halo.shape[0]) * LANES
    return pl.pallas_call(
        gradient_kernel,
        out_shape=(
            jax.ShapeDtypeStruct((11, blocks, LANES), jnp.float32),
            jax.ShapeDtypeStruct((blocks, SUB, LANES), jnp.float32),
        ),
        in_specs=[SMEM, SMEM] + [VMEM] * 7,
        out_specs=(VMEM, VMEM),
        scratch_shapes=[
            pltpu.VMEM((7, space, LANES), jnp.float32),
            pltpu.VMEM((13, blocks, LANES), jnp.float32),
        ],
        compiler_params=params(),
    )(table, count, own, halo, halo_density, smooth, mass, energy, first)


def force_kernel(table, count, own_ref, halo_ref, near_ref, halo_near_ref, out_ref, wide_ref):
    blocks = own_ref.shape[0]
    halos = halo_ref.shape[0]
    spread_all(lambda b: own_ref[b], blocks, 0, wide_ref, 0, (0, 1, 2))
    spread_all(lambda b: halo_ref[b], halos, blocks, wide_ref, 0, (0, 1, 2))
    spread_all(lambda b: near_ref[b], blocks, 0, wide_ref, 3, tuple(range(7)))
    spread_all(lambda b: halo_near_ref[b], halos, blocks, wide_ref, 3, tuple(range(7)))

    def prepare(b):
        return [full(own_ref[b, f : f + 1, :]) for f in range(3)]

    def load(at):
        return [wide_ref[n, at, :] for n in range(10)]

    def pair(c, here, sums):
        d = [c[a] - here[a] for a in range(3)]
        square = d[0] * d[0] + d[1] * d[1] + d[2] * d[2]
        w = profile(square * c[9])
        x, y, z = (w * d[a] for a in range(3))
        return (
            sums[0] + c[3] * x + c[4] * y + c[5] * z,
            sums[1] + c[4] * x + c[6] * y + c[7] * z,
            sums[2] + c[5] * x + c[7] * y + c[8] * z,
        )

    sweep(table, count, blocks, 3, load, prepare, pair, out_ref)


def force_call(table, count, own, halo, near, halo_near):
    blocks = own.shape[0]
    space = (blocks + halo.shape[0]) * LANES
    return pl.pallas_call(
        force_kernel,
        out_shape=jax.ShapeDtypeStruct((3, blocks, LANES), jnp.float32),
        in_specs=[SMEM, SMEM] + [VMEM] * 4,
        out_specs=VMEM,
        scratch_shapes=[pltpu.VMEM((10, space, LANES), jnp.float32)],
        compiler_params=params(),
    )(table, count, own, halo, near, halo_near)


SENT = 21
ROWS = 29


def pack_kernel(place_ref, fields_ref, out_ref, slots_ref, rows_ref):
    count, blocks = fields_ref.shape[0], fields_ref.shape[1]
    owners = out_ref.shape[0]
    span = 3 * count

    def clear(i, carry):
        slots_ref[pl.ds(pl.multiple_of(i * 128, 128), 128), :] = jnp.zeros((128, LANES), jnp.float32)
        return carry

    lax.fori_loop(0, slots_ref.shape[0] // 128, clear, 0)
    row, col = (lax.broadcasted_iota(jnp.int32, (span, LANES), n) for n in (0, 1))
    same = (row == col).astype(jnp.float32).astype(jnp.bfloat16)
    group = 8

    def turn(g, carry):
        rows = [
            jnp.concatenate([fields_ref[f, pl.ds(g * group + i, 1), :] for f in range(count)], axis=0) for i in range(group)
        ]
        x = jnp.concatenate(rows, axis=1)
        high = x.astype(jnp.bfloat16).astype(jnp.float32)
        middle = (x - high).astype(jnp.bfloat16).astype(jnp.float32)
        parts = jnp.concatenate([high, middle, x - high - middle], axis=0).astype(jnp.bfloat16)
        at = pl.ds(pl.multiple_of(g * group * LANES, group * LANES), group * LANES)
        rows_ref[at, :] = lax.dot_general(parts, same, (((0,), (0,)), ((), ())), preferred_element_type=jnp.float32)
        return carry

    lax.fori_loop(0, blocks // group, turn, 0)

    def scatter(b, carry):
        start = pl.multiple_of(b * LANES, LANES)
        for i in range(LANES):
            slots_ref[pl.ds(place_ref[b * LANES + i], 1), :] = rows_ref[pl.ds(start + i, 1), :]
        return carry

    lax.fori_loop(0, blocks, scatter, 0)
    row, col = (lax.broadcasted_iota(jnp.int32, (count, LANES), n) for n in (0, 1))
    gather = ((lax.rem(col, count) == row) & (col < span)).astype(jnp.float32).astype(jnp.bfloat16)

    def turned(at, length):
        rows = slots_ref[pl.ds(at, length), :].astype(jnp.bfloat16)
        return lax.dot_general(gather, rows, (((1,), (1,)), ((), ())), preferred_element_type=jnp.float32)

    def main(g, carry):
        out = turned(pl.multiple_of(g * group * MAIN, MAIN), group * MAIN)
        for i in range(group):
            piece = out[:, i * LANES : (i + 1) * LANES]
            out_ref[g * group + i, 0:16, :] = piece[0:16]
            out_ref[g * group + i, 24:ROWS, :] = piece[16:SENT]
        return carry

    lax.fori_loop(0, owners // group, main, 0)
    lane = lax.broadcasted_iota(jnp.int32, (SUB, LANES), 1) // REST

    def rest(g, carry):
        out = turned(pl.multiple_of(owners * MAIN + g * LANES, LANES), LANES)
        for i in range(LANES // REST):
            mixed = jnp.zeros((SUB, LANES), jnp.float32)
            for v in range(count // SUB):
                piece = out[v * SUB : (v + 1) * SUB, :]
                shift = (v - i) * REST % LANES
                if shift:
                    piece = pltpu.roll(piece, shift, 1)
                mixed = jnp.where(lane == v, piece, mixed)
            out_ref[g * (LANES // REST) + i, 16:24, :] = mixed
        return carry

    lax.fori_loop(0, owners * REST // LANES, rest, 0)


def pack_call(place, fields, owners):
    blocks = fields.shape[1]
    return pl.pallas_call(
        pack_kernel,
        out_shape=jax.ShapeDtypeStruct((owners, ROWS, LANES), jnp.float32),
        in_specs=[SMEM, VMEM],
        out_specs=VMEM,
        scratch_shapes=[
            pltpu.VMEM((owners * (MAIN + REST), LANES), jnp.float32),
            pltpu.VMEM((blocks * LANES, LANES), jnp.float32),
        ],
        compiler_params=params(),
    )(place, fields)


def migrate_kernel(step_ref, in_ref, out_ref, inbox, send_sem, recv_sem):
    sources = in_ref.shape[0]
    slab, rank = lax.axis_index("slab"), lax.axis_index("ranges")
    barrier = pltpu.get_barrier_semaphore()

    def hello(t, carry):
        pl.semaphore_signal(barrier, inc=1, device_id=(slab, lax.rem(rank + t, sources)), device_id_type=MESH)
        return carry

    lax.fori_loop(1, sources, hello, 0)
    pl.semaphore_wait(barrier, sources - 1)

    def copy(t):
        to = lax.rem(rank + t, sources)
        return pltpu.make_async_remote_copy(
            src_ref=in_ref.at[to],
            dst_ref=inbox.at[rank],
            send_sem=send_sem.at[t],
            recv_sem=recv_sem.at[rank],
            device_id=(slab, to),
            device_id_type=MESH,
        )

    def send(t, carry):
        copy(t).start()
        return carry

    lax.fori_loop(1, sources, send, 0)
    pltpu.make_async_copy(in_ref.at[rank], inbox.at[rank], recv_sem.at[rank]).start()
    lane = lax.broadcasted_iota(jnp.int32, (SUB, LANES), 1)
    step = step_ref[0]
    slots = MAIN + REST

    def arrived(q):
        pltpu.make_async_copy(in_ref.at[q], inbox.at[q], recv_sem.at[q]).wait()

    def lay(n, carry):
        g = lax.rem(rank // 4 + sources // 4 - 1 - n, sources // 4)
        for i in range(4):
            arrived(g * 4 + i)
        made = []
        for v, at in enumerate((0, 8, 24)):
            high = min(at + SUB, ROWS)
            columns = [None] * 5
            for i in range(4):
                first = inbox[g * 4 + i, at:high, :]
                last = inbox[g * 4 + i, 16 : 16 + high - at, :]
                place = lane[0 : high - at]
                c, off = i * slots // LANES, i * slots % LANES
                moved = pltpu.roll(first, off, 1) if off else first
                columns[c] = jnp.where(place < off, columns[c], moved) if off else moved
                if off:
                    columns[c + 1] = moved
                c = c + 1
                shift = (off - v * REST) % LANES
                moved = pltpu.roll(last, shift, 1) if shift else last
                columns[c] = jnp.where(place < off, columns[c], moved) if off else moved
            made.append(columns)
        for c in range(5):
            low, top, more = (columns[c] for columns in made)
            density, heating, energy = low[6:7], top[5:6], top[6:7]
            cols = pl.ds(pl.multiple_of(g * 5 * LANES + c * LANES, LANES), LANES)
            out_ref[0:6, cols] = low[0:6]
            out_ref[6:7, cols] = more[4:5]
            out_ref[7:8, cols] = low[7:8]
            out_ref[8:9, cols] = energy + step * heating
            out_ref[9:10, cols] = density
            out_ref[10:11, cols] = (GAMMA - 1.0) * density * energy
            out_ref[11:12, cols] = jnp.sqrt(GAMMA * (GAMMA - 1.0) * energy)
            out_ref[12:16, cols] = more[0:4]
            out_ref[16:24, cols] = top
        return carry

    lax.fori_loop(0, sources // 4, lay, 0)

    def sent(t, carry):
        copy(t).wait_send()
        return carry

    lax.fori_loop(1, sources, sent, 0)


def migrate_call(step_size, packed):
    sources = packed.shape[0]
    return pl.pallas_call(
        migrate_kernel,
        out_shape=jax.ShapeDtypeStruct((24, sources * (MAIN + REST)), jnp.float32),
        in_specs=[SMEM, VMEM],
        out_specs=VMEM,
        scratch_shapes=[
            pltpu.VMEM(packed.shape, jnp.float32),
            pltpu.SemaphoreType.DMA((sources,)),
            pltpu.SemaphoreType.DMA((sources,)),
        ],
        compiler_params=params(collective_id=4, has_side_effects=True),
    )(step_size.reshape(1), packed)


def slot_rows(keys, owners):
    owner = lax.rem(keys // KEY_SPAN, owners)
    blocks = owner.shape[0]
    onehot = (owner[:, None, :] == jnp.arange(owners)[None, :, None]).astype(jnp.bfloat16)
    before = (jnp.arange(LANES)[:, None] < jnp.arange(LANES)[None, :]).astype(jnp.bfloat16)
    inside = jnp.einsum("bok,kl->bol", onehot, before, preferred_element_type=jnp.float32)
    totals = jnp.sum(onehot.astype(jnp.float32), axis=2)
    earlier = (jnp.arange(blocks)[:, None] > jnp.arange(blocks)[None, :]).astype(jnp.float32)
    ahead = jnp.dot(earlier, totals, precision=lax.Precision.HIGHEST)
    rank = jnp.sum(onehot.astype(jnp.float32) * (inside + ahead[:, :, None]), axis=1).astype(jnp.int32)
    return jnp.where(rank < MAIN, owner * MAIN + rank, owners * MAIN + owner * REST + rank - MAIN)


def per_device(state, keys, halo_list, neighbour_block_table, neighbour_block_count):
    blocks = neighbour_block_table.shape[0]
    owners = lax.axis_size("ranges")
    table = neighbour_block_table.reshape(-1)
    count = neighbour_block_count
    rows = state.reshape(state.shape[0], blocks, LANES)
    position, velocity, smooth, mass, energy = rows[0:3], rows[3:6], rows[6], rows[7], rows[8]
    own = jnp.transpose(rows[0:8], (1, 0, 2))
    speed = jnp.sqrt(jnp.sum(velocity * velocity, axis=0))
    sound = jnp.sqrt(GAMMA * (GAMMA - 1.0) * energy)
    least = jnp.full((SUB, LANES), jnp.min(smooth / (sound + speed)), jnp.float32)
    place = slot_rows(keys.reshape(blocks, LANES), owners).reshape(-1)

    halo, least = exchange_call(own, halo_list, least, 0)
    first = density_call(table, count, own, halo, smooth)
    density = first[0]
    halo_density, least = exchange_call(density[:, None, :], halo_list, least, 1)
    coef, near = gradient_call(table, count, own, halo, halo_density[:, 0, :], smooth, mass, energy, first)
    halo_near, least = exchange_call(near, halo_list, least, 2)
    step_size = COURANT * least[0, 0]
    pull = force_call(table, count, own, halo, near, halo_near)

    acceleration = -(coef[7:10] + pull)
    vel_new = velocity + step_size * acceleration
    smooth_new = SMOOTH_ETA * jnp.cbrt(mass / density)
    fields = jnp.concatenate(
        [
            position + step_size * vel_new,
            vel_new,
            density[None],
            mass[None],
            coef[4:6],
            acceleration,
            coef[10:11],
            energy[None],
            coef[6:7],
            coef[0:4],
            smooth_new[None],
            jnp.zeros((3,) + energy.shape, energy.dtype),
        ],
        axis=0,
    )
    return (migrate_call(step_size, pack_call(place, fields, owners)), step_size)


def solution(mesh):
    both = ("slab", "ranges")
    return jax.shard_map(
        per_device,
        mesh=mesh,
        in_specs=(P(None, both), P(both), P(both), P(both, None), P(both)),
        out_specs=(P(None, both), P()),
        check_vma=False,
    )
```

```python
import functools

import jax
import jax.numpy as jnp
from jax import lax
from jax.experimental import pallas as pl
from jax.experimental.pallas import tpu as pltpu
from jax.sharding import PartitionSpec as P

KEY_SPAN = 2048
GAMMA = 5.0 / 3.0
COURANT = 0.3
SMOOTH_ETA = 1.2
REGULAR = 0.02

LANES = 128
SUB = 8
TILES = 4
TERMS = 7
FIRST = (0, 1, 2, 3, 4, 5, 7)
MAIN = 128
REST = 32
TINY = 1e-30
FAR = 4.0
MESH = pl.DeviceIdType.MESH
VMEM = pl.BlockSpec(memory_space=pltpu.VMEM)
SMEM = pl.BlockSpec(memory_space=pltpu.SMEM)


def params(mebibytes, **more):
    return pltpu.CompilerParams(vmem_limit_bytes=mebibytes * 1024 * 1024, **more)


def curve_neighbours():
    slabs, ranges = lax.axis_size("slab"), lax.axis_size("ranges")
    me = lax.axis_index("slab") * ranges + lax.axis_index("ranges")
    after = lax.rem(me + 1, slabs * ranges)
    before = lax.rem(me + slabs * ranges - 1, slabs * ranges)
    return [(d // ranges, lax.rem(d, ranges)) for d in (before, after)]


def swap_halo(own_ref, lists, packed, landed, send_sem, recv_sem, span):
    before, after = curve_neighbours()
    first = lists.shape[0] - 2 * span
    for i in range(2 * span):
        packed[i] = own_ref[lists[first + i]]
    copies = []
    for side, target in ((0, before), (1, after)):
        copy = pltpu.make_async_remote_copy(
            src_ref=packed.at[pl.ds(side * span, span)],
            dst_ref=landed.at[pl.ds((1 - side) * span, span)],
            send_sem=send_sem.at[side],
            recv_sem=recv_sem.at[side],
            device_id=target,
            device_id_type=MESH,
        )
        copy.start()
        copies.append(copy)
    return copies


def greet(partners):
    barrier = pltpu.get_barrier_semaphore()
    for partner in partners:
        pl.semaphore_signal(barrier, inc=1, device_id=partner, device_id_type=MESH)
    return lambda: pl.semaphore_wait(barrier, len(partners))


def slab_partners():
    slabs = lax.axis_size("slab")
    slab, rank = lax.axis_index("slab"), lax.axis_index("ranges")
    return [(lax.rem(slab + t, slabs), rank) for t in range(1, slabs)]


def slot_rows(owner, owners, place_ref):
    blocks = owner.shape[0]
    row, col = (lax.broadcasted_iota(jnp.int32, (LANES, LANES), n) for n in (0, 1))
    upto = (row <= col).astype(jnp.float32).astype(jnp.bfloat16)
    kind = lax.broadcasted_iota(jnp.int32, (owners, LANES), 0)
    ahead = jnp.zeros((owners, 1), jnp.float32)
    for b in range(blocks):
        mine = owner[b : b + 1, :]
        same = (kind == mine).astype(jnp.float32)
        seen = jnp.dot(same.astype(jnp.bfloat16), upto, preferred_element_type=jnp.float32)
        rank = jnp.sum(same * (seen + ahead), axis=0, keepdims=True).astype(jnp.int32) - 1
        ahead = ahead + seen[:, LANES - 1 :]
        place_ref[b : b + 1, :] = jnp.where(
            rank < MAIN, mine * MAIN + rank, owners * MAIN + mine * REST + rank - MAIN
        )


def first_kernel(
    span,
    owners,
    lists,
    state_ref,
    keys_ref,
    halo_ref,
    rows_ref,
    own_ref,
    min_ref,
    place_ref,
    *refs,
):
    wide, (packed, landed, send_sem, recv_sem, least, inbox, put_sem, got_sem) = refs[:TERMS], refs[TERMS:]
    partners = slab_partners()
    wait = greet(curve_neighbours() + partners)
    blocks = own_ref.shape[0]

    def block(b):
        return state_ref[0:SUB, pl.ds(pl.multiple_of(b * LANES, LANES), LANES)]

    for b in range(blocks):
        for f in range(rows_ref.shape[0]):
            rows_ref[f, b : b + 1, :] = state_ref[f : f + 1, b * LANES : (b + 1) * LANES]
    total = rows_ref[3] * rows_ref[3] + rows_ref[4] * rows_ref[4] + rows_ref[5] * rows_ref[5]
    sound = jnp.sqrt(GAMMA * (GAMMA - 1.0) * rows_ref[8])
    least[...] = jnp.full((SUB, LANES), jnp.min(rows_ref[6] / (sound + jnp.sqrt(total))), jnp.float32)
    for b in range(blocks):
        own_ref[b] = block(b)
    wait()
    copies = swap_halo(own_ref, lists, packed, landed, send_sem, recv_sem, span)
    small = []
    for slot, partner in enumerate(partners):
        copy = pltpu.make_async_remote_copy(
            src_ref=least,
            dst_ref=inbox.at[slot],
            send_sem=put_sem.at[slot],
            recv_sem=got_sem.at[slot],
            device_id=partner,
            device_id_type=MESH,
        )
        copy.start()
        small.append(copy)
    spread_all(block, blocks, 0, tuple(zip(wide, FIRST)))
    slot_rows(lax.rem(keys_ref[...] // KEY_SPAN, owners), owners, place_ref)
    for copy in copies:
        copy.wait()
    halo_ref[...] = landed[...]
    value = least[...]
    for slot, copy in enumerate(small):
        copy.wait()
        value = jnp.minimum(value, inbox[slot])
    min_ref[0] = value[0:1]


def first_call(lists, state, keys, span, owners):
    blocks = keys.shape[0]
    slabs = lax.axis_size("slab")
    shape = (2 * span, SUB, LANES)
    space = (blocks + 2 * span) * LANES
    return pl.pallas_call(
        functools.partial(first_kernel, span, owners),
        out_shape=(
            jax.ShapeDtypeStruct(shape, jnp.float32),
            jax.ShapeDtypeStruct((state.shape[0], blocks, LANES), jnp.float32),
            jax.ShapeDtypeStruct((blocks, SUB, LANES), jnp.float32),
            jax.ShapeDtypeStruct((1, 1, LANES), jnp.float32),
            jax.ShapeDtypeStruct((blocks, LANES), jnp.int32),
        )
        + (jax.ShapeDtypeStruct((space, LANES), jnp.float32),) * TERMS,
        in_specs=[SMEM, VMEM, VMEM],
        out_specs=(VMEM,) * (5 + TERMS),
        scratch_shapes=[
            pltpu.VMEM(shape, jnp.float32),
            pltpu.VMEM(shape, jnp.float32),
            pltpu.SemaphoreType.DMA((2,)),
            pltpu.SemaphoreType.DMA((2,)),
            pltpu.VMEM((SUB, LANES), jnp.float32),
            pltpu.VMEM((slabs - 1, SUB, LANES), jnp.float32),
            pltpu.SemaphoreType.DMA((slabs - 1,)),
            pltpu.SemaphoreType.DMA((slabs - 1,)),
        ],
        compiler_params=params(4, collective_id=1, has_side_effects=True),
    )(lists, state, keys)


def density_halo_kernel(
    span, lists, first_ref, own_ref, halo_ref, volume_ref, packed, landed, send_sem, recv_sem, density
):
    wait = greet(curve_neighbours())
    blocks = own_ref.shape[0]
    for b in range(blocks):
        density[b] = first_ref[0, b : b + 1, :]
    wait()
    copies = swap_halo(density, lists, packed, landed, send_sem, recv_sem, span)
    spread_all(
        lambda b: with_volume(own_ref[b], density[b]), blocks, 0, ((volume_ref, 7),)
    )
    for copy in copies:
        copy.wait()
    halo_ref[...] = landed[...]


def density_halo_call(lists, first, own, span):
    blocks = own.shape[0]
    shape = (2 * span, 1, LANES)
    return pl.pallas_call(
        functools.partial(density_halo_kernel, span),
        out_shape=(
            jax.ShapeDtypeStruct(shape, jnp.float32),
            jax.ShapeDtypeStruct(((blocks + 2 * span) * LANES, LANES), jnp.float32),
        ),
        in_specs=[SMEM, VMEM, VMEM],
        out_specs=(VMEM, VMEM),
        scratch_shapes=[
            pltpu.VMEM(shape, jnp.float32),
            pltpu.VMEM(shape, jnp.float32),
            pltpu.SemaphoreType.DMA((2,)),
            pltpu.SemaphoreType.DMA((2,)),
            pltpu.VMEM((blocks, 1, LANES), jnp.float32),
        ],
        compiler_params=params(4, collective_id=2, has_side_effects=True),
    )(lists, first, own)


def near_halo_kernel(span, lists, near_ref, halo_ref, *refs):
    greet(curve_neighbours())()
    more, (packed, landed, send_sem, recv_sem) = refs[:TERMS], refs[TERMS:]
    copies = swap_halo(near_ref, lists, packed, landed, send_sem, recv_sem, span)
    spread_all(lambda b: near_ref[b], near_ref.shape[0], 0, tuple((ref, n) for n, ref in enumerate(more)))
    for copy in copies:
        copy.wait()
    halo_ref[...] = landed[...]


def near_halo_call(lists, near, span):
    blocks = near.shape[0]
    shape = (2 * span, SUB, LANES)
    return pl.pallas_call(
        functools.partial(near_halo_kernel, span),
        out_shape=(jax.ShapeDtypeStruct(shape, jnp.float32),)
        + (jax.ShapeDtypeStruct(((blocks + 2 * span) * LANES, LANES), jnp.float32),) * TERMS,
        in_specs=[SMEM, VMEM],
        out_specs=(VMEM,) * (1 + TERMS),
        scratch_shapes=[
            pltpu.VMEM(shape, jnp.float32),
            pltpu.VMEM(shape, jnp.float32),
            pltpu.SemaphoreType.DMA((2,)),
            pltpu.SemaphoreType.DMA((2,)),
        ],
        compiler_params=params(4, collective_id=3, has_side_effects=True),
    )(lists, near)


def spread(rows, start, targets):
    x = jnp.concatenate(rows, axis=1)
    high = x.astype(jnp.bfloat16).astype(jnp.float32)
    middle = (x - high).astype(jnp.bfloat16).astype(jnp.float32)
    parts = jnp.concatenate([high, middle, x - high - middle], axis=0).astype(jnp.bfloat16)
    kind = lax.rem(lax.broadcasted_iota(jnp.int32, (3 * SUB, LANES), 0), SUB)
    at = pl.ds(pl.multiple_of(start * LANES, LANES), x.shape[1])
    for i in range(0, len(targets), 2):
        pair = targets[i : i + 2]
        pick = jnp.concatenate([(kind == f).astype(jnp.float32).astype(jnp.bfloat16) for _, f in pair], axis=1)
        out = lax.dot_general(parts, pick, (((0,), (0,)), ((), ())), preferred_element_type=jnp.float32)
        for m, (ref, _) in enumerate(pair):
            ref[at, :] = out[:, m * LANES : (m + 1) * LANES]


def spread_all(make, count, first, targets, group=10):
    def turn(g, carry):
        spread([make(g * group + i) for i in range(group)], first + g * group, targets)
        return carry

    lax.fori_loop(0, count // group, turn, 0)


def profile(square):
    near = jnp.minimum(square, FAR)
    ratio = near * lax.rsqrt(jnp.maximum(near, TINY))
    outer = jnp.maximum(2.0 - ratio, 0.0)
    inner = jnp.maximum(outer - 1.0, 0.0)
    return outer * outer * (0.25 * outer) - inner * inner * inner


def full(row):
    return jnp.broadcast_to(row, (SUB, LANES))


def shear(w, u):
    return (
        u[0] * w[0],
        u[0] * w[1] + u[1] * w[0],
        u[0] * w[2] + u[2] * w[0],
        u[1] * w[1],
        u[1] * w[2] + u[2] * w[1],
        u[2] * w[2],
    )


def sweep(lists, blocks, width, load, prepare, pair, sums_ref):
    tiles = TILES

    def block(b, carry):
        here = prepare(b)

        def tile(k, sums):
            start = lists[b * tiles + k] * LANES
            for s in range(LANES // SUB):
                at = pl.ds(pl.multiple_of(start + s * SUB, SUB), SUB)
                kept = pl.ds(pl.multiple_of((b * tiles + k) * LANES + s * SUB, SUB), SUB)
                sums = pair(load(at), here, sums, kept)
            return sums

        zero = jnp.zeros((SUB, LANES), jnp.float32)
        sums = lax.fori_loop(0, lists[tiles * blocks + b], tile, (zero,) * width)
        for f in range(width):
            sums_ref[f, pl.ds(b, 1), :] = jnp.sum(sums[f], axis=0, keepdims=True)
        return carry

    lax.fori_loop(0, blocks, block, 0)


def add(sums, terms):
    return tuple(s + t for s, t in zip(sums, terms))


def density_kernel(lists, own_ref, halo_ref, smooth_ref, *refs):
    out_ref, kept_ref, wide = refs[TERMS], refs[TERMS + 1], refs[TERMS + 2 :]
    blocks, halos = own_ref.shape[0], halo_ref.shape[0]
    spread_all(lambda b: halo_ref[b], halos, blocks, tuple(zip(wide, FIRST)))

    def prepare(b):
        h = own_ref[b, 6:7, :]
        return [full(own_ref[b, f : f + 1, :]) for f in range(6)] + [full(1.0 / (h * h))]

    def load(at):
        return [ref[at, :] for ref in wide]

    def pair(c, here, sums, kept):
        d = [c[a] - here[a] for a in range(3)]
        square = d[0] * d[0] + d[1] * d[1] + d[2] * d[2]
        w = profile(square * here[6])
        kept_ref[kept, :] = w
        w = w * c[6]
        wd = [w * d[a] for a in range(3)]
        u = [c[3 + a] - here[3 + a] for a in range(3)]
        return add(sums, (w, *wd, *shear(wd, u)))

    sweep(lists, blocks, 10, load, prepare, pair, out_ref)
    h = smooth_ref[...]
    norm = 1.0 / (jnp.pi * h * h * h)
    for f in range(10):
        out_ref[f] = out_ref[f] * norm


def density_call(lists, own, halo, smooth, wide):
    blocks = own.shape[0]
    return pl.pallas_call(
        density_kernel,
        out_shape=(
            jax.ShapeDtypeStruct((10, blocks, LANES), jnp.float32),
            jax.ShapeDtypeStruct((TILES * blocks * LANES, LANES), jnp.float32),
        )
        + tuple(jax.ShapeDtypeStruct(part.shape, jnp.float32) for part in wide),
        in_specs=[SMEM] + [VMEM] * (3 + TERMS),
        out_specs=(VMEM,) * (2 + TERMS),
        input_output_aliases={4 + n: 2 + n for n in range(TERMS)},
        compiler_params=params(4),
    )(lists, own, halo, smooth, *wide)


def with_volume(rows, density):
    return jnp.concatenate([rows[0:7], rows[7:8] / density], axis=0)


def gradient_kernel(
    lists,
    own_ref,
    halo_ref,
    halo_density_ref,
    smooth_ref,
    mass_ref,
    energy_ref,
    first_ref,
    kept_ref,
    volume_in,
    *refs,
):
    wide, (coef_ref, near_ref, volume_ref, sums_ref) = refs[:6], refs[6:]
    blocks = own_ref.shape[0]

    spread_all(
        lambda b: with_volume(halo_ref[b], halo_density_ref[b]), halo_ref.shape[0], blocks, ((volume_ref, 7),)
    )

    def prepare(b):
        return [full(own_ref[b, f : f + 1, :]) for f in range(6)]

    def load(at):
        return [ref[at, :] for ref in (*wide, volume_ref)]

    def pair(c, here, sums, kept):
        w = kept_ref[kept, :] * c[6]
        d = [c[a] - here[a] for a in range(3)]
        wd = [w * d[a] for a in range(3)]
        u = [c[3 + a] - here[3 + a] for a in range(3)]
        tau = (wd[0] * d[0], wd[0] * d[1], wd[0] * d[2], wd[1] * d[1], wd[1] * d[2], wd[2] * d[2])
        return add(sums, (w, *tau, *shear(wd, u)))

    sweep(lists, blocks, 13, load, prepare, pair, sums_ref)
    h = smooth_ref[...]
    norm = 1.0 / (jnp.pi * h * h * h)
    s = [sums_ref[f] * norm for f in range(13)]
    diagonal = REGULAR * h * h * s[0]
    xx, xy, xz, yy, yz, zz = s[1] + diagonal, s[2], s[3], s[4] + diagonal, s[5], s[6] + diagonal
    cof = (
        yy * zz - yz * yz,
        xz * yz - xy * zz,
        xy * yz - xz * yy,
        xx * zz - xz * xz,
        xy * xz - xx * yz,
        xx * yy - xy * xy,
    )
    determinant = xx * cof[0] + xy * cof[1] + xz * cof[2]
    coef = [c / determinant for c in cof]
    divergence = sum(c * t for c, t in zip(coef, s[7:13]))
    density = first_ref[0]
    factor = (GAMMA - 1.0) * density * energy_ref[...] / (density * density)
    heating = -factor * sum(coef[n] * first_ref[4 + n] for n in range(6))
    pull = [first_ref[1 + a] for a in range(3)]
    own_part = [
        factor * (coef[0] * pull[0] + coef[1] * pull[1] + coef[2] * pull[2]),
        factor * (coef[1] * pull[0] + coef[3] * pull[1] + coef[4] * pull[2]),
        factor * (coef[2] * pull[0] + coef[4] * pull[1] + coef[5] * pull[2]),
    ]
    for n, value in enumerate([*coef, divergence, *own_part, heating]):
        coef_ref[n] = value
    scale = mass_ref[...] * factor * norm
    inverse = 1.0 / (h * h)
    for n in range(6):
        sums_ref[n] = coef[n] * scale
    sums_ref[6] = inverse
    sums_ref[7] = inverse

    def regroup(b, carry):
        near_ref[b] = jnp.concatenate([sums_ref[n, pl.ds(b, 1), :] for n in range(8)], axis=0)
        return carry

    lax.fori_loop(0, blocks, regroup, 0)


def gradient_call(lists, own, halo, halo_density, smooth, mass, energy, first, kept, volume, wide):
    blocks = own.shape[0]
    return pl.pallas_call(
        gradient_kernel,
        out_shape=(
            jax.ShapeDtypeStruct((11, blocks, LANES), jnp.float32),
            jax.ShapeDtypeStruct((blocks, SUB, LANES), jnp.float32),
            jax.ShapeDtypeStruct(volume.shape, jnp.float32),
        ),
        in_specs=[SMEM] + [VMEM] * 15,
        out_specs=(VMEM,) * 3,
        input_output_aliases={9: 2},
        scratch_shapes=[pltpu.VMEM((13, blocks, LANES), jnp.float32)],
        compiler_params=params(4),
    )(lists, own, halo, halo_density, smooth, mass, energy, first, kept, volume, *wide)


def force_kernel(lists, own_ref, halo_near_ref, *refs):
    wide, out_ref, more = refs[:3], refs[3 + TERMS], refs[4 + TERMS :]
    blocks, halos = own_ref.shape[0], halo_near_ref.shape[0]
    spread_all(lambda b: halo_near_ref[b], halos, blocks, tuple((ref, n) for n, ref in enumerate(more)))

    def prepare(b):
        return [full(own_ref[b, f : f + 1, :]) for f in range(3)]

    def load(at):
        return [ref[at, :] for ref in (*wide, *more)]

    def pair(c, here, sums, kept):
        d = [c[a] - here[a] for a in range(3)]
        square = d[0] * d[0] + d[1] * d[1] + d[2] * d[2]
        w = profile(square * c[9])
        x, y, z = (w * d[a] for a in range(3))
        return (
            sums[0] + c[3] * x + c[4] * y + c[5] * z,
            sums[1] + c[4] * x + c[6] * y + c[7] * z,
            sums[2] + c[5] * x + c[7] * y + c[8] * z,
        )

    sweep(lists, blocks, 3, load, prepare, pair, out_ref)


def force_call(lists, own, halo_near, wide, more):
    blocks = own.shape[0]
    return pl.pallas_call(
        force_kernel,
        out_shape=(jax.ShapeDtypeStruct((3, blocks, LANES), jnp.float32),)
        + tuple(jax.ShapeDtypeStruct(part.shape, jnp.float32) for part in more),
        in_specs=[SMEM] + [VMEM] * (5 + TERMS),
        out_specs=(VMEM,) * (1 + TERMS),
        input_output_aliases={6 + n: 1 + n for n in range(TERMS)},
        compiler_params=params(4),
    )(lists, own, halo_near, *wide, *more)


SENT = 20
PIECE = 5
ROWS = SENT + PIECE


def pack_kernel(place_ref, state_ref, first_ref, coef_ref, pull_ref, out_ref, slots_ref, rows_ref, fields_ref):
    values = [state_ref[f] for f in range(6)] + [first_ref[0], state_ref[7], coef_ref[4], coef_ref[5]]
    values = values + [-(coef_ref[7 + a] + pull_ref[a]) for a in range(3)] + [coef_ref[10], state_ref[8], coef_ref[6]]
    values = values + [coef_ref[n] for n in range(4)]
    for f, value in enumerate(values):
        fields_ref[f] = value
    for f in range(SENT, fields_ref.shape[0]):
        fields_ref[f] = jnp.zeros(fields_ref.shape[1:], jnp.float32)
    count, blocks = fields_ref.shape[0], fields_ref.shape[1]
    owners = out_ref.shape[0]
    span = 3 * count

    def clear(i, carry):
        slots_ref[pl.ds(pl.multiple_of(i * 128, 128), 128), :] = jnp.zeros((128, LANES), jnp.float32)
        return carry

    lax.fori_loop(0, slots_ref.shape[0] // 128, clear, 0)
    row, col = (lax.broadcasted_iota(jnp.int32, (span, LANES), n) for n in (0, 1))
    same = (row == col).astype(jnp.float32).astype(jnp.bfloat16)
    group = 8

    def turn(g, carry):
        rows = [
            jnp.concatenate([fields_ref[f, pl.ds(g * group + i, 1), :] for f in range(count)], axis=0) for i in range(group)
        ]
        x = jnp.concatenate(rows, axis=1)
        high = x.astype(jnp.bfloat16).astype(jnp.float32)
        middle = (x - high).astype(jnp.bfloat16).astype(jnp.float32)
        parts = jnp.concatenate([high, middle, x - high - middle], axis=0).astype(jnp.bfloat16)
        at = pl.ds(pl.multiple_of(g * group * LANES, group * LANES), group * LANES)
        rows_ref[at, :] = lax.dot_general(parts, same, (((0,), (0,)), ((), ())), preferred_element_type=jnp.float32)
        return carry

    lax.fori_loop(0, blocks // group, turn, 0)

    def scatter(b, carry):
        start = pl.multiple_of(b * LANES, LANES)
        for i in range(LANES):
            slots_ref[pl.ds(place_ref[b * LANES + i], 1), :] = rows_ref[pl.ds(start + i, 1), :]
        return carry

    lax.fori_loop(0, blocks, scatter, 0)
    row, col = (lax.broadcasted_iota(jnp.int32, (count, LANES), n) for n in (0, 1))
    gather = ((lax.rem(col, count) == row) & (col < span)).astype(jnp.float32).astype(jnp.bfloat16)

    def turned(at, length):
        rows = slots_ref[pl.ds(at, length), :].astype(jnp.bfloat16)
        return lax.dot_general(gather, rows, (((1,), (1,)), ((), ())), preferred_element_type=jnp.float32)

    def main(g, carry):
        out = turned(pl.multiple_of(g * group * MAIN, MAIN), group * MAIN)
        for i in range(group):
            piece = out[:, i * LANES : (i + 1) * LANES]
            out_ref[g * group + i, 0:SENT, :] = piece[0:SENT]
        return carry

    lax.fori_loop(0, owners // group, main, 0)
    lane = lax.broadcasted_iota(jnp.int32, (PIECE, LANES), 1) // REST

    def rest(g, carry):
        out = turned(pl.multiple_of(owners * MAIN + g * LANES, LANES), LANES)
        for i in range(LANES // REST):
            mixed = jnp.zeros((PIECE, LANES), jnp.float32)
            for v in range(SENT // PIECE):
                piece = out[v * PIECE : (v + 1) * PIECE, :]
                shift = (v - i) * REST % LANES
                if shift:
                    piece = pltpu.roll(piece, shift, 1)
                mixed = jnp.where(lane == v, piece, mixed)
            out_ref[g * (LANES // REST) + i, SENT:ROWS, :] = mixed
        return carry

    lax.fori_loop(0, owners * REST // LANES, rest, 0)


def pack_call(place, state, first, coef, pull, owners):
    blocks = state.shape[1]
    return pl.pallas_call(
        pack_kernel,
        out_shape=jax.ShapeDtypeStruct((owners, ROWS, LANES), jnp.float32),
        in_specs=[SMEM] + [VMEM] * 4,
        out_specs=VMEM,
        scratch_shapes=[
            pltpu.VMEM((owners * (MAIN + REST), LANES), jnp.float32),
            pltpu.VMEM((blocks * LANES, LANES), jnp.float32),
            pltpu.VMEM((24, blocks, LANES), jnp.float32),
        ],
        compiler_params=params(12),
    )(place, state, first, coef, pull)


def cube_root(value):
    size = jnp.abs(value)
    some = size > 0.0
    safe = jnp.where(some, size, 1.0)
    root = jnp.exp(jnp.log(safe) * (1.0 / 3.0))
    root = root - (root - safe / (root * root)) * (1.0 / 3.0)
    return jnp.where(some, jnp.where(value < 0.0, -root, root), 0.0)


def migrate_kernel(in_ref, least_ref, out_ref, step_ref, inbox, minima, send_sem, recv_sem, put_sem, got_sem):
    sources = in_ref.shape[0]
    slab, rank = lax.axis_index("slab"), lax.axis_index("ranges")
    barrier = pltpu.get_barrier_semaphore()

    def hello(t, carry):
        pl.semaphore_signal(barrier, inc=1, device_id=(slab, lax.rem(rank + t, sources)), device_id_type=MESH)
        return carry

    lax.fori_loop(1, sources, hello, 0)
    pl.semaphore_wait(barrier, sources - 1)

    def copy(t):
        to = lax.rem(rank + t, sources)
        return pltpu.make_async_remote_copy(
            src_ref=in_ref.at[to],
            dst_ref=inbox.at[rank],
            send_sem=send_sem.at[t],
            recv_sem=recv_sem.at[rank],
            device_id=(slab, to),
            device_id_type=MESH,
        )

    def tell(t):
        to = lax.rem(rank + t, sources)
        return pltpu.make_async_remote_copy(
            src_ref=least_ref.at[0],
            dst_ref=minima.at[rank],
            send_sem=put_sem.at[t],
            recv_sem=got_sem.at[rank],
            device_id=(slab, to),
            device_id_type=MESH,
        )

    def send(t, carry):
        tell(t).start()
        copy(t).start()
        return carry

    lax.fori_loop(1, sources, send, 0)
    pltpu.make_async_copy(in_ref.at[rank], inbox.at[rank], recv_sem.at[rank]).start()
    pltpu.make_async_copy(least_ref.at[0], minima.at[rank], got_sem.at[rank]).start()
    lane = lax.broadcasted_iota(jnp.int32, (SUB, LANES), 1)
    slots = MAIN + REST

    def lay(n, carry):
        g = lax.rem(rank // 4 + sources // 4 - 1 - n, sources // 4)
        for i in range(4):
            q = g * 4 + i
            pltpu.make_async_copy(in_ref.at[q], inbox.at[q], recv_sem.at[q]).wait()
        made = [[None] * 5 for v in range(3)]
        for i in range(4):
            q = g * 4 + i
            c, off = i * slots // LANES, i * slots % LANES
            pieces = []
            last = inbox[q, SENT:ROWS, :]
            for v in range(SENT // PIECE):
                shift = (off - v * REST) % LANES
                pieces.append(pltpu.roll(last, shift, 1) if shift else last)
            rest = jnp.concatenate(pieces, axis=0)
            for v, at in enumerate((0, 8, 16)):
                high = min(at + SUB, SENT)
                columns = made[v]
                place = lane[0 : high - at]
                first = inbox[q, at:high, :]
                moved = pltpu.roll(first, off, 1) if off else first
                columns[c] = jnp.where(place < off, columns[c], moved) if off else moved
                tail = rest[at:high]
                columns[c + 1] = jnp.where(place < off, moved, tail) if off else tail
        for c in range(5):
            low, top, more = (columns[c] for columns in made)
            density, mass, energy = low[6:7], low[7:8], top[6:7]
            ratio = jnp.where(density != 0.0, mass / density, 0.0)
            cols = pl.ds(pl.multiple_of(g * 5 * LANES + c * LANES, LANES), LANES)
            out_ref[0:6, cols] = low[0:6]
            out_ref[6:7, cols] = SMOOTH_ETA * cube_root(ratio)
            out_ref[7:8, cols] = mass
            out_ref[9:10, cols] = density
            out_ref[10:11, cols] = (GAMMA - 1.0) * density * energy
            out_ref[11:12, cols] = jnp.sqrt(GAMMA * (GAMMA - 1.0) * energy)
            out_ref[12:16, cols] = more
            out_ref[16:24, cols] = top
        return carry

    lax.fori_loop(0, sources // 4, lay, 0)

    def hear(q, carry):
        pltpu.make_async_copy(least_ref.at[0], minima.at[q], got_sem.at[q]).wait()
        return carry

    lax.fori_loop(0, sources, hear, 0)
    step = COURANT * jnp.min(minima[...])
    step_ref[...] = jnp.full(step_ref.shape, step, jnp.float32)

    def advance(c, carry):
        cols = pl.ds(pl.multiple_of(c * LANES, LANES), LANES)
        speed = out_ref[3:6, cols] + step * out_ref[18:21, cols]
        out_ref[3:6, cols] = speed
        out_ref[0:3, cols] = out_ref[0:3, cols] + step * speed
        out_ref[8:9, cols] = out_ref[22:23, cols] + step * out_ref[21:22, cols]
        return carry

    lax.fori_loop(0, out_ref.shape[1] // LANES, advance, 0, unroll=4)

    def sent(t, carry):
        copy(t).wait_send()
        tell(t).wait_send()
        return carry

    lax.fori_loop(1, sources, sent, 0)


def migrate_call(packed, least):
    sources = packed.shape[0]
    return pl.pallas_call(
        migrate_kernel,
        out_shape=(
            jax.ShapeDtypeStruct((24, sources * (MAIN + REST)), jnp.float32),
            jax.ShapeDtypeStruct((SUB, LANES), jnp.float32),
        ),
        in_specs=[VMEM, VMEM],
        out_specs=(VMEM, VMEM),
        scratch_shapes=[
            pltpu.VMEM(packed.shape, jnp.float32),
            pltpu.VMEM((sources, 1, LANES), jnp.float32),
            pltpu.SemaphoreType.DMA((sources,)),
            pltpu.SemaphoreType.DMA((sources,)),
            pltpu.SemaphoreType.DMA((sources,)),
            pltpu.SemaphoreType.DMA((sources,)),
        ],
        compiler_params=params(12, collective_id=4, has_side_effects=True),
    )(packed, least)


def per_device(state, keys, halo_list, neighbour_block_table, neighbour_block_count):
    blocks = neighbour_block_table.shape[0]
    owners = lax.axis_size("ranges")
    lists = jnp.concatenate([neighbour_block_table.reshape(-1), neighbour_block_count, halo_list])
    span = halo_list.shape[0] // 2

    halo, rows, own, least, place, *wide = first_call(lists, state, keys.reshape(blocks, LANES), span, owners)
    smooth, mass, energy = rows[6], rows[7], rows[8]
    first, kept, *wide = density_call(lists, own, halo, smooth, wide)
    halo_density, volume = density_halo_call(lists, first, own, span)
    coef, near, _ = gradient_call(
        lists, own, halo, halo_density, smooth, mass, energy, first, kept, volume, wide[:6]
    )
    halo_near, *more = near_halo_call(lists, near, span)
    pull, *_ = force_call(lists, own, halo_near, wide[:3], more)
    packed = pack_call(place.reshape(-1), rows, first, coef, pull, owners)
    migrated, step = migrate_call(packed, least)
    return (migrated, step[0, 0])


def solution(mesh):
    both = ("slab", "ranges")
    return jax.shard_map(
        per_device,
        mesh=mesh,
        in_specs=(P(None, both), P(both), P(both), P(both, None), P(both)),
        out_specs=(P(None, both), P()),
        check_vma=False,
    )
```

```python
import functools

import jax
import jax.numpy as jnp
from jax import lax
from jax.experimental import pallas as pl
from jax.experimental.pallas import tpu as pltpu
from jax.sharding import PartitionSpec as P

KEY_SPAN = 2048
GAMMA = 5.0 / 3.0
COURANT = 0.3
SMOOTH_ETA = 1.2
REGULAR = 0.02

LANES = 128
SUB = 8
TILES = 4
TERMS = 7
FIRST = (0, 1, 2, 3, 4, 5, 7)
MAIN = 128
REST = 32
TINY = 1e-30
FAR = 4.0
MESH = pl.DeviceIdType.MESH
VMEM = pl.BlockSpec(memory_space=pltpu.VMEM)
SMEM = pl.BlockSpec(memory_space=pltpu.SMEM)


def params(mebibytes, **more):
    return pltpu.CompilerParams(vmem_limit_bytes=mebibytes * 1024 * 1024, **more)


def curve_neighbours():
    slabs, ranges = lax.axis_size("slab"), lax.axis_size("ranges")
    me = lax.axis_index("slab") * ranges + lax.axis_index("ranges")
    after = lax.rem(me + 1, slabs * ranges)
    before = lax.rem(me + slabs * ranges - 1, slabs * ranges)
    return [(d // ranges, lax.rem(d, ranges)) for d in (before, after)]


def swap_halo(own_ref, lists, packed, landed, send_sem, recv_sem, span):
    before, after = curve_neighbours()
    first = lists.shape[0] - 2 * span
    for i in range(2 * span):
        packed[i] = own_ref[lists[first + i]]
    copies = []
    for side, target in ((0, before), (1, after)):
        copy = pltpu.make_async_remote_copy(
            src_ref=packed.at[pl.ds(side * span, span)],
            dst_ref=landed.at[pl.ds((1 - side) * span, span)],
            send_sem=send_sem.at[side],
            recv_sem=recv_sem.at[side],
            device_id=target,
            device_id_type=MESH,
        )
        copy.start()
        copies.append(copy)
    return copies


def greet(partners):
    barrier = pltpu.get_barrier_semaphore()
    for partner in partners:
        pl.semaphore_signal(barrier, inc=1, device_id=partner, device_id_type=MESH)
    return lambda: pl.semaphore_wait(barrier, len(partners))


def slab_partners():
    slabs = lax.axis_size("slab")
    slab, rank = lax.axis_index("slab"), lax.axis_index("ranges")
    return [(lax.rem(slab + t, slabs), rank) for t in range(1, slabs)]


def slot_rows(owner, owners, place_ref):
    blocks = owner.shape[0]
    row, col = (lax.broadcasted_iota(jnp.int32, (LANES, LANES), n) for n in (0, 1))
    upto = (row <= col).astype(jnp.float32).astype(jnp.bfloat16)
    kind = lax.broadcasted_iota(jnp.int32, (owners, LANES), 0)
    ahead = jnp.zeros((owners, 1), jnp.float32)
    for b in range(blocks):
        mine = owner[b : b + 1, :]
        same = (kind == mine).astype(jnp.float32)
        seen = jnp.dot(same.astype(jnp.bfloat16), upto, preferred_element_type=jnp.float32)
        rank = jnp.sum(same * (seen + ahead), axis=0, keepdims=True).astype(jnp.int32) - 1
        ahead = ahead + seen[:, LANES - 1 :]
        place_ref[b : b + 1, :] = jnp.where(
            rank < MAIN, mine * MAIN + rank, owners * MAIN + mine * REST + rank - MAIN
        )


def first_kernel(
    span,
    owners,
    lists,
    state_ref,
    keys_ref,
    halo_ref,
    rows_ref,
    own_ref,
    min_ref,
    place_ref,
    *refs,
):
    wide, (packed, landed, send_sem, recv_sem, least, inbox, put_sem, got_sem) = refs[:TERMS], refs[TERMS:]
    partners = slab_partners()
    wait = greet(curve_neighbours() + partners)
    blocks = own_ref.shape[0]

    def block(b):
        return state_ref[0:SUB, pl.ds(pl.multiple_of(b * LANES, LANES), LANES)]

    for b in range(blocks):
        for f in range(rows_ref.shape[0]):
            rows_ref[f, b : b + 1, :] = state_ref[f : f + 1, b * LANES : (b + 1) * LANES]
    total = rows_ref[3] * rows_ref[3] + rows_ref[4] * rows_ref[4] + rows_ref[5] * rows_ref[5]
    sound = jnp.sqrt(GAMMA * (GAMMA - 1.0) * rows_ref[8])
    least[...] = jnp.full((SUB, LANES), jnp.min(rows_ref[6] / (sound + jnp.sqrt(total))), jnp.float32)
    for b in range(blocks):
        own_ref[b] = block(b)
    wait()
    copies = swap_halo(own_ref, lists, packed, landed, send_sem, recv_sem, span)
    small = []
    for slot, partner in enumerate(partners):
        copy = pltpu.make_async_remote_copy(
            src_ref=least,
            dst_ref=inbox.at[slot],
            send_sem=put_sem.at[slot],
            recv_sem=got_sem.at[slot],
            device_id=partner,
            device_id_type=MESH,
        )
        copy.start()
        small.append(copy)
    spread_all(block, blocks, 0, tuple(zip(wide, FIRST)))
    slot_rows(lax.rem(keys_ref[...] // KEY_SPAN, owners), owners, place_ref)
    for copy in copies:
        copy.wait()
    halo_ref[...] = landed[...]
    value = least[...]
    for slot, copy in enumerate(small):
        copy.wait()
        value = jnp.minimum(value, inbox[slot])
    min_ref[0] = value[0:1]


def first_call(lists, state, keys, span, owners):
    blocks = keys.shape[0]
    slabs = lax.axis_size("slab")
    shape = (2 * span, SUB, LANES)
    space = (blocks + 2 * span) * LANES
    return pl.pallas_call(
        functools.partial(first_kernel, span, owners),
        out_shape=(
            jax.ShapeDtypeStruct(shape, jnp.float32),
            jax.ShapeDtypeStruct((state.shape[0], blocks, LANES), jnp.float32),
            jax.ShapeDtypeStruct((blocks, SUB, LANES), jnp.float32),
            jax.ShapeDtypeStruct((1, 1, LANES), jnp.float32),
            jax.ShapeDtypeStruct((blocks, LANES), jnp.int32),
        )
        + (jax.ShapeDtypeStruct((space, LANES), jnp.float32),) * TERMS,
        in_specs=[SMEM, VMEM, VMEM],
        out_specs=(VMEM,) * (5 + TERMS),
        scratch_shapes=[
            pltpu.VMEM(shape, jnp.float32),
            pltpu.VMEM(shape, jnp.float32),
            pltpu.SemaphoreType.DMA((2,)),
            pltpu.SemaphoreType.DMA((2,)),
            pltpu.VMEM((SUB, LANES), jnp.float32),
            pltpu.VMEM((slabs - 1, SUB, LANES), jnp.float32),
            pltpu.SemaphoreType.DMA((slabs - 1,)),
            pltpu.SemaphoreType.DMA((slabs - 1,)),
        ],
        compiler_params=params(4, collective_id=1, has_side_effects=True),
    )(lists, state, keys)


def density_halo_kernel(span, lists, first_ref, own_ref, kept_ref, *refs):
    wide, (halo_ref, volume_ref, part_ref, packed, landed, send_sem, recv_sem, density) = refs[:6], refs[6:]
    wait = greet(curve_neighbours())
    blocks = own_ref.shape[0]
    for b in range(blocks):
        density[b] = first_ref[0, b : b + 1, :]
    wait()
    copies = swap_halo(density, lists, packed, landed, send_sem, recv_sem, span)
    spread_all(lambda b: with_volume(own_ref[b], density[b]), blocks, 0, ((volume_ref, 7),))
    prepare, load, pair = gradient_parts(own_ref, kept_ref, (*wide, volume_ref))

    def block(b, carry):
        sums = (jnp.zeros((SUB, LANES), jnp.float32),) * part_ref.shape[0]
        sums = one_tile(b * LANES, b * TILES * LANES, load, prepare(b), pair, sums)
        for f, value in enumerate(sums):
            part_ref[f, b] = value
        return carry

    lax.fori_loop(0, blocks, block, 0)
    for copy in copies:
        copy.wait()
    halo_ref[...] = landed[...]


def density_halo_call(lists, first, own, span, kept, wide):
    blocks = own.shape[0]
    shape = (2 * span, 1, LANES)
    return pl.pallas_call(
        functools.partial(density_halo_kernel, span),
        out_shape=(
            jax.ShapeDtypeStruct(shape, jnp.float32),
            jax.ShapeDtypeStruct(((blocks + 2 * span) * LANES, LANES), jnp.float32),
            jax.ShapeDtypeStruct((13, blocks, SUB, LANES), jnp.float32),
        ),
        in_specs=[SMEM] + [VMEM] * 9,
        out_specs=(VMEM, VMEM, VMEM),
        scratch_shapes=[
            pltpu.VMEM(shape, jnp.float32),
            pltpu.VMEM(shape, jnp.float32),
            pltpu.SemaphoreType.DMA((2,)),
            pltpu.SemaphoreType.DMA((2,)),
            pltpu.VMEM((blocks, 1, LANES), jnp.float32),
        ],
        compiler_params=params(4, collective_id=2, has_side_effects=True),
    )(lists, first, own, kept, *wide)


def near_halo_kernel(span, lists, near_ref, halo_ref, *refs):
    greet(curve_neighbours())()
    more, (packed, landed, send_sem, recv_sem) = refs[:TERMS], refs[TERMS:]
    copies = swap_halo(near_ref, lists, packed, landed, send_sem, recv_sem, span)
    spread_all(lambda b: near_ref[b], near_ref.shape[0], 0, tuple((ref, n) for n, ref in enumerate(more)))
    for copy in copies:
        copy.wait()
    halo_ref[...] = landed[...]


def near_halo_call(lists, near, span):
    blocks = near.shape[0]
    shape = (2 * span, SUB, LANES)
    return pl.pallas_call(
        functools.partial(near_halo_kernel, span),
        out_shape=(jax.ShapeDtypeStruct(shape, jnp.float32),)
        + (jax.ShapeDtypeStruct(((blocks + 2 * span) * LANES, LANES), jnp.float32),) * TERMS,
        in_specs=[SMEM, VMEM],
        out_specs=(VMEM,) * (1 + TERMS),
        scratch_shapes=[
            pltpu.VMEM(shape, jnp.float32),
            pltpu.VMEM(shape, jnp.float32),
            pltpu.SemaphoreType.DMA((2,)),
            pltpu.SemaphoreType.DMA((2,)),
        ],
        compiler_params=params(4, collective_id=3, has_side_effects=True),
    )(lists, near)


def spread(rows, start, targets):
    x = jnp.concatenate(rows, axis=1)
    high = x.astype(jnp.bfloat16).astype(jnp.float32)
    middle = (x - high).astype(jnp.bfloat16).astype(jnp.float32)
    parts = jnp.concatenate([high, middle, x - high - middle], axis=0).astype(jnp.bfloat16)
    kind = lax.rem(lax.broadcasted_iota(jnp.int32, (3 * SUB, LANES), 0), SUB)
    at = pl.ds(pl.multiple_of(start * LANES, LANES), x.shape[1])
    for i in range(0, len(targets), 2):
        pair = targets[i : i + 2]
        pick = jnp.concatenate([(kind == f).astype(jnp.float32).astype(jnp.bfloat16) for _, f in pair], axis=1)
        out = lax.dot_general(parts, pick, (((0,), (0,)), ((), ())), preferred_element_type=jnp.float32)
        for m, (ref, _) in enumerate(pair):
            ref[at, :] = out[:, m * LANES : (m + 1) * LANES]


def spread_all(make, count, first, targets, group=10):
    def turn(g, carry):
        spread([make(g * group + i) for i in range(group)], first + g * group, targets)
        return carry

    lax.fori_loop(0, count // group, turn, 0)


def profile(square):
    near = jnp.minimum(square, FAR)
    ratio = near * lax.rsqrt(jnp.maximum(near, TINY))
    outer = jnp.maximum(2.0 - ratio, 0.0)
    inner = jnp.maximum(outer - 1.0, 0.0)
    return outer * outer * (0.25 * outer) - inner * inner * inner


def full(row):
    return jnp.broadcast_to(row, (SUB, LANES))


def shear(w, u):
    return (
        u[0] * w[0],
        u[0] * w[1] + u[1] * w[0],
        u[0] * w[2] + u[2] * w[0],
        u[1] * w[1],
        u[1] * w[2] + u[2] * w[1],
        u[2] * w[2],
    )


def one_tile(start, kept, load, here, pair, sums):
    for s in range(LANES // SUB):
        at = pl.ds(pl.multiple_of(start + s * SUB, SUB), SUB)
        sums = pair(load(at), here, sums, pl.ds(pl.multiple_of(kept + s * SUB, SUB), SUB))
    return sums


def sweep(lists, blocks, width, load, prepare, pair, sums_ref, part_ref=None):
    def block(b, carry):
        here = prepare(b)

        def tile(k, sums):
            return one_tile(lists[b * TILES + k] * LANES, (b * TILES + k) * LANES, load, here, pair, sums)

        if part_ref is None:
            first, sums = 0, (jnp.zeros((SUB, LANES), jnp.float32),) * width
        else:
            first, sums = 1, tuple(part_ref[f, b] for f in range(width))
        sums = lax.fori_loop(first, lists[TILES * blocks + b], tile, sums)
        for f in range(width):
            sums_ref[f, pl.ds(b, 1), :] = jnp.sum(sums[f], axis=0, keepdims=True)
        return carry

    lax.fori_loop(0, blocks, block, 0)


def add(sums, terms):
    return tuple(s + t for s, t in zip(sums, terms))


def density_kernel(lists, own_ref, halo_ref, smooth_ref, *refs):
    out_ref, kept_ref, *wide = refs[TERMS:]
    blocks, halos = own_ref.shape[0], halo_ref.shape[0]
    spread_all(lambda b: halo_ref[b], halos, blocks, tuple(zip(wide, FIRST)))

    def prepare(b):
        h = own_ref[b, 6:7, :]
        return [full(own_ref[b, f : f + 1, :]) for f in range(6)] + [full(1.0 / (h * h))]

    def load(at):
        return [ref[at, :] for ref in wide]

    def pair(c, here, sums, kept):
        d = [c[a] - here[a] for a in range(3)]
        square = d[0] * d[0] + d[1] * d[1] + d[2] * d[2]
        w = profile(square * here[6])
        kept_ref[kept, :] = w
        w = w * c[6]
        wd = [w * d[a] for a in range(3)]
        u = [c[3 + a] - here[3 + a] for a in range(3)]
        return add(sums, (w, *wd, *shear(wd, u)))

    sweep(lists, blocks, 10, load, prepare, pair, out_ref)
    h = smooth_ref[...]
    norm = 1.0 / (jnp.pi * h * h * h)
    for f in range(10):
        out_ref[f] = out_ref[f] * norm


def density_call(lists, own, halo, smooth, wide):
    blocks = own.shape[0]
    return pl.pallas_call(
        density_kernel,
        out_shape=(
            jax.ShapeDtypeStruct((10, blocks, LANES), jnp.float32),
            jax.ShapeDtypeStruct((TILES * blocks * LANES, LANES), jnp.float32),
        )
        + tuple(jax.ShapeDtypeStruct(part.shape, jnp.float32) for part in wide),
        in_specs=[SMEM] + [VMEM] * (3 + TERMS),
        out_specs=(VMEM,) * (2 + TERMS),
        input_output_aliases={4 + n: 2 + n for n in range(TERMS)},
        compiler_params=params(4),
    )(lists, own, halo, smooth, *wide)


def with_volume(rows, density):
    return jnp.concatenate([rows[0:7], rows[7:8] / density], axis=0)


def gradient_parts(own_ref, kept_ref, columns):
    def prepare(b):
        return [full(own_ref[b, f : f + 1, :]) for f in range(6)]

    def load(at):
        return [ref[at, :] for ref in columns]

    def pair(c, here, sums, kept):
        w = kept_ref[kept, :] * c[6]
        d = [c[a] - here[a] for a in range(3)]
        wd = [w * d[a] for a in range(3)]
        u = [c[3 + a] - here[3 + a] for a in range(3)]
        tau = (wd[0] * d[0], wd[0] * d[1], wd[0] * d[2], wd[1] * d[1], wd[1] * d[2], wd[2] * d[2])
        return add(sums, (w, *tau, *shear(wd, u)))

    return prepare, load, pair


def gradient_kernel(
    lists,
    own_ref,
    halo_ref,
    halo_density_ref,
    smooth_ref,
    mass_ref,
    energy_ref,
    first_ref,
    kept_ref,
    part_ref,
    volume_in,
    *refs,
):
    wide, (coef_ref, near_ref, volume_ref, sums_ref) = refs[:6], refs[6:]
    blocks = own_ref.shape[0]

    spread_all(
        lambda b: with_volume(halo_ref[b], halo_density_ref[b]), halo_ref.shape[0], blocks, ((volume_ref, 7),)
    )

    prepare, load, pair = gradient_parts(own_ref, kept_ref, (*wide, volume_ref))
    sweep(lists, blocks, 13, load, prepare, pair, sums_ref, part_ref)
    h = smooth_ref[...]
    norm = 1.0 / (jnp.pi * h * h * h)
    s = [sums_ref[f] * norm for f in range(13)]
    diagonal = REGULAR * h * h * s[0]
    xx, xy, xz, yy, yz, zz = s[1] + diagonal, s[2], s[3], s[4] + diagonal, s[5], s[6] + diagonal
    cof = (
        yy * zz - yz * yz,
        xz * yz - xy * zz,
        xy * yz - xz * yy,
        xx * zz - xz * xz,
        xy * xz - xx * yz,
        xx * yy - xy * xy,
    )
    determinant = xx * cof[0] + xy * cof[1] + xz * cof[2]
    coef = [c / determinant for c in cof]
    divergence = sum(c * t for c, t in zip(coef, s[7:13]))
    density = first_ref[0]
    factor = (GAMMA - 1.0) * density * energy_ref[...] / (density * density)
    heating = -factor * sum(coef[n] * first_ref[4 + n] for n in range(6))
    pull = [first_ref[1 + a] for a in range(3)]
    own_part = [
        factor * (coef[0] * pull[0] + coef[1] * pull[1] + coef[2] * pull[2]),
        factor * (coef[1] * pull[0] + coef[3] * pull[1] + coef[4] * pull[2]),
        factor * (coef[2] * pull[0] + coef[4] * pull[1] + coef[5] * pull[2]),
    ]
    for n, value in enumerate([*coef, divergence, *own_part, heating]):
        coef_ref[n] = value
    scale = mass_ref[...] * factor * norm
    inverse = 1.0 / (h * h)
    for n in range(6):
        sums_ref[n] = coef[n] * scale
    sums_ref[6] = inverse
    sums_ref[7] = inverse

    def regroup(b, carry):
        near_ref[b] = jnp.concatenate([sums_ref[n, pl.ds(b, 1), :] for n in range(8)], axis=0)
        return carry

    lax.fori_loop(0, blocks, regroup, 0)


def gradient_call(lists, own, halo, halo_density, smooth, mass, energy, first, kept, part, volume, wide):
    blocks = own.shape[0]
    return pl.pallas_call(
        gradient_kernel,
        out_shape=(
            jax.ShapeDtypeStruct((11, blocks, LANES), jnp.float32),
            jax.ShapeDtypeStruct((blocks, SUB, LANES), jnp.float32),
            jax.ShapeDtypeStruct(volume.shape, jnp.float32),
        ),
        in_specs=[SMEM] + [VMEM] * 16,
        out_specs=(VMEM,) * 3,
        input_output_aliases={10: 2},
        scratch_shapes=[pltpu.VMEM((13, blocks, LANES), jnp.float32)],
        compiler_params=params(4),
    )(lists, own, halo, halo_density, smooth, mass, energy, first, kept, part, volume, *wide)


def force_kernel(lists, own_ref, halo_near_ref, *refs):
    wide, (out_ref, *more) = refs[:3], refs[3 + TERMS :]
    blocks, halos = own_ref.shape[0], halo_near_ref.shape[0]
    spread_all(lambda b: halo_near_ref[b], halos, blocks, tuple((ref, n) for n, ref in enumerate(more)))

    def prepare(b):
        return [full(own_ref[b, f : f + 1, :]) for f in range(3)]

    def load(at):
        return [ref[at, :] for ref in (*wide, *more)]

    def pair(c, here, sums, kept):
        d = [c[a] - here[a] for a in range(3)]
        square = d[0] * d[0] + d[1] * d[1] + d[2] * d[2]
        w = profile(square * c[9])
        x, y, z = (w * d[a] for a in range(3))
        return (
            sums[0] + c[3] * x + c[4] * y + c[5] * z,
            sums[1] + c[4] * x + c[6] * y + c[7] * z,
            sums[2] + c[5] * x + c[7] * y + c[8] * z,
        )

    sweep(lists, blocks, 3, load, prepare, pair, out_ref)


def force_call(lists, own, halo_near, wide, more):
    blocks = own.shape[0]
    return pl.pallas_call(
        force_kernel,
        out_shape=(jax.ShapeDtypeStruct((3, blocks, LANES), jnp.float32),)
        + tuple(jax.ShapeDtypeStruct(part.shape, jnp.float32) for part in more),
        in_specs=[SMEM] + [VMEM] * (5 + TERMS),
        out_specs=(VMEM,) * (1 + TERMS),
        input_output_aliases={6 + n: 1 + n for n in range(TERMS)},
        compiler_params=params(4),
    )(lists, own, halo_near, *wide, *more)


SENT = 20
PIECE = 5
ROWS = SENT + PIECE


def pack_kernel(place_ref, state_ref, first_ref, coef_ref, pull_ref, out_ref, slots_ref, rows_ref, fields_ref):
    values = [state_ref[f] for f in range(6)] + [first_ref[0], state_ref[7], coef_ref[4], coef_ref[5]]
    values = values + [-(coef_ref[7 + a] + pull_ref[a]) for a in range(3)] + [coef_ref[10], state_ref[8], coef_ref[6]]
    values = values + [coef_ref[n] for n in range(4)]
    for f, value in enumerate(values):
        fields_ref[f] = value
    for f in range(SENT, fields_ref.shape[0]):
        fields_ref[f] = jnp.zeros(fields_ref.shape[1:], jnp.float32)
    count, blocks = fields_ref.shape[0], fields_ref.shape[1]
    owners = out_ref.shape[0]
    span = 3 * count

    def clear(i, carry):
        slots_ref[pl.ds(pl.multiple_of(i * 128, 128), 128), :] = jnp.zeros((128, LANES), jnp.float32)
        return carry

    lax.fori_loop(0, slots_ref.shape[0] // 128, clear, 0)
    row, col = (lax.broadcasted_iota(jnp.int32, (span, LANES), n) for n in (0, 1))
    same = (row == col).astype(jnp.float32).astype(jnp.bfloat16)
    group = 8

    def turn(g, carry):
        rows = [
            jnp.concatenate([fields_ref[f, pl.ds(g * group + i, 1), :] for f in range(count)], axis=0) for i in range(group)
        ]
        x = jnp.concatenate(rows, axis=1)
        high = x.astype(jnp.bfloat16).astype(jnp.float32)
        middle = (x - high).astype(jnp.bfloat16).astype(jnp.float32)
        parts = jnp.concatenate([high, middle, x - high - middle], axis=0).astype(jnp.bfloat16)
        at = pl.ds(pl.multiple_of(g * group * LANES, group * LANES), group * LANES)
        rows_ref[at, :] = lax.dot_general(parts, same, (((0,), (0,)), ((), ())), preferred_element_type=jnp.float32)
        return carry

    lax.fori_loop(0, blocks // group, turn, 0)

    def scatter(b, carry):
        start = pl.multiple_of(b * LANES, LANES)
        for i in range(LANES):
            slots_ref[pl.ds(place_ref[b * LANES + i], 1), :] = rows_ref[pl.ds(start + i, 1), :]
        return carry

    lax.fori_loop(0, blocks, scatter, 0)
    row, col = (lax.broadcasted_iota(jnp.int32, (count, LANES), n) for n in (0, 1))
    gather = ((lax.rem(col, count) == row) & (col < span)).astype(jnp.float32).astype(jnp.bfloat16)

    def turned(at, length):
        rows = slots_ref[pl.ds(at, length), :].astype(jnp.bfloat16)
        return lax.dot_general(gather, rows, (((1,), (1,)), ((), ())), preferred_element_type=jnp.float32)

    def main(g, carry):
        out = turned(pl.multiple_of(g * group * MAIN, MAIN), group * MAIN)
        for i in range(group):
            piece = out[:, i * LANES : (i + 1) * LANES]
            out_ref[g * group + i, 0:SENT, :] = piece[0:SENT]
        return carry

    lax.fori_loop(0, owners // group, main, 0)
    lane = lax.broadcasted_iota(jnp.int32, (PIECE, LANES), 1) // REST

    quarters = LANES // REST
    batch = group * LANES

    def rest(g, carry):
        out = turned(pl.multiple_of(owners * MAIN + g * batch, batch), batch)
        for j in range(group):
            part = out[:, j * LANES : (j + 1) * LANES]
            for i in range(quarters):
                mixed = jnp.zeros((PIECE, LANES), jnp.float32)
                for v in range(SENT // PIECE):
                    piece = part[v * PIECE : (v + 1) * PIECE, :]
                    shift = (v - i) * REST % LANES
                    if shift:
                        piece = pltpu.roll(piece, shift, 1)
                    mixed = jnp.where(lane == v, piece, mixed)
                out_ref[(g * group + j) * quarters + i, SENT:ROWS, :] = mixed
        return carry

    lax.fori_loop(0, owners * REST // batch, rest, 0)


def pack_call(place, state, first, coef, pull, owners):
    blocks = state.shape[1]
    return pl.pallas_call(
        pack_kernel,
        out_shape=jax.ShapeDtypeStruct((owners, ROWS, LANES), jnp.float32),
        in_specs=[SMEM] + [VMEM] * 4,
        out_specs=VMEM,
        scratch_shapes=[
            pltpu.VMEM((owners * (MAIN + REST), LANES), jnp.float32),
            pltpu.VMEM((blocks * LANES, LANES), jnp.float32),
            pltpu.VMEM((24, blocks, LANES), jnp.float32),
        ],
        compiler_params=params(12),
    )(place, state, first, coef, pull)


def cube_root(value):
    size = jnp.abs(value)
    some = size > 0.0
    safe = jnp.where(some, size, 1.0)
    root = jnp.exp(jnp.log(safe) * (1.0 / 3.0))
    root = root - (root - safe / (root * root)) * (1.0 / 3.0)
    return jnp.where(some, jnp.where(value < 0.0, -root, root), 0.0)


def migrate_kernel(in_ref, least_ref, out_ref, step_ref, inbox, minima, send_sem, recv_sem, put_sem, got_sem):
    sources = in_ref.shape[0]
    slab, rank = lax.axis_index("slab"), lax.axis_index("ranges")
    barrier = pltpu.get_barrier_semaphore()

    def hello(t, carry):
        pl.semaphore_signal(barrier, inc=1, device_id=(slab, lax.rem(rank + t, sources)), device_id_type=MESH)
        return carry

    lax.fori_loop(1, sources, hello, 0)
    pl.semaphore_wait(barrier, sources - 1)

    def copy(t):
        to = lax.rem(rank + t, sources)
        return pltpu.make_async_remote_copy(
            src_ref=in_ref.at[to],
            dst_ref=inbox.at[rank],
            send_sem=send_sem.at[t],
            recv_sem=recv_sem.at[rank],
            device_id=(slab, to),
            device_id_type=MESH,
        )

    def tell(t):
        to = lax.rem(rank + t, sources)
        return pltpu.make_async_remote_copy(
            src_ref=least_ref.at[0],
            dst_ref=minima.at[rank],
            send_sem=put_sem.at[t],
            recv_sem=got_sem.at[rank],
            device_id=(slab, to),
            device_id_type=MESH,
        )

    def send(t, carry):
        tell(t).start()
        copy(t).start()
        return carry

    lax.fori_loop(1, sources, send, 0)
    pltpu.make_async_copy(in_ref.at[rank], inbox.at[rank], recv_sem.at[rank]).start()
    pltpu.make_async_copy(least_ref.at[0], minima.at[rank], got_sem.at[rank]).start()
    lane = lax.broadcasted_iota(jnp.int32, (SUB, LANES), 1)
    slots = MAIN + REST

    def lay(n, carry):
        g = lax.rem(rank // 4 + sources // 4 - 1 - n, sources // 4)
        for i in range(4):
            q = g * 4 + i
            pltpu.make_async_copy(in_ref.at[q], inbox.at[q], recv_sem.at[q]).wait()
        made = [[None] * 5 for v in range(3)]
        for i in range(4):
            q = g * 4 + i
            c, off = i * slots // LANES, i * slots % LANES
            pieces = []
            last = inbox[q, SENT:ROWS, :]
            for v in range(SENT // PIECE):
                shift = (off - v * REST) % LANES
                pieces.append(pltpu.roll(last, shift, 1) if shift else last)
            rest = jnp.concatenate(pieces, axis=0)
            for v, at in enumerate((0, 8, 16)):
                high = min(at + SUB, SENT)
                columns = made[v]
                place = lane[0 : high - at]
                first = inbox[q, at:high, :]
                moved = pltpu.roll(first, off, 1) if off else first
                columns[c] = jnp.where(place < off, columns[c], moved) if off else moved
                tail = rest[at:high]
                columns[c + 1] = jnp.where(place < off, moved, tail) if off else tail
        for c in range(5):
            low, top, more = (columns[c] for columns in made)
            density, mass, energy = low[6:7], low[7:8], top[6:7]
            ratio = jnp.where(density != 0.0, mass / density, 0.0)
            cols = pl.ds(pl.multiple_of(g * 5 * LANES + c * LANES, LANES), LANES)
            out_ref[0:6, cols] = low[0:6]
            out_ref[6:7, cols] = SMOOTH_ETA * cube_root(ratio)
            out_ref[7:8, cols] = mass
            out_ref[9:10, cols] = density
            out_ref[10:11, cols] = (GAMMA - 1.0) * density * energy
            out_ref[11:12, cols] = jnp.sqrt(GAMMA * (GAMMA - 1.0) * energy)
            out_ref[12:16, cols] = more
            out_ref[16:24, cols] = top
        return carry

    lax.fori_loop(0, sources // 4, lay, 0)

    def hear(q, carry):
        pltpu.make_async_copy(least_ref.at[0], minima.at[q], got_sem.at[q]).wait()
        return carry

    lax.fori_loop(0, sources, hear, 0)
    step = COURANT * jnp.min(minima[...])
    step_ref[0] = step

    def advance(c, carry):
        cols = pl.ds(pl.multiple_of(c * LANES, LANES), LANES)
        speed = out_ref[3:6, cols] + step * out_ref[18:21, cols]
        out_ref[3:6, cols] = speed
        out_ref[0:3, cols] = out_ref[0:3, cols] + step * speed
        out_ref[8:9, cols] = out_ref[22:23, cols] + step * out_ref[21:22, cols]
        return carry

    lax.fori_loop(0, out_ref.shape[1] // LANES, advance, 0, unroll=4)

    def sent(t, carry):
        copy(t).wait_send()
        tell(t).wait_send()
        return carry

    lax.fori_loop(1, sources, sent, 0)


def migrate_call(packed, least):
    sources = packed.shape[0]
    return pl.pallas_call(
        migrate_kernel,
        out_shape=(
            jax.ShapeDtypeStruct((24, sources * (MAIN + REST)), jnp.float32),
            jax.ShapeDtypeStruct((1,), jnp.float32),
        ),
        in_specs=[VMEM, VMEM],
        out_specs=(VMEM, SMEM),
        scratch_shapes=[
            pltpu.VMEM(packed.shape, jnp.float32),
            pltpu.VMEM((sources, 1, LANES), jnp.float32),
            pltpu.SemaphoreType.DMA((sources,)),
            pltpu.SemaphoreType.DMA((sources,)),
            pltpu.SemaphoreType.DMA((sources,)),
            pltpu.SemaphoreType.DMA((sources,)),
        ],
        compiler_params=params(12, collective_id=4, has_side_effects=True),
    )(packed, least)


def per_device(state, keys, halo_list, neighbour_block_table, neighbour_block_count):
    blocks = neighbour_block_table.shape[0]
    owners = lax.axis_size("ranges")
    lists = jnp.concatenate([neighbour_block_table.reshape(-1), neighbour_block_count, halo_list])
    span = halo_list.shape[0] // 2

    halo, rows, own, least, place, *wide = first_call(lists, state, keys.reshape(blocks, LANES), span, owners)
    smooth, mass, energy = rows[6], rows[7], rows[8]
    first, kept, *wide = density_call(lists, own, halo, smooth, wide)
    halo_density, volume, part = density_halo_call(lists, first, own, span, kept, wide[:6])
    coef, near, _ = gradient_call(
        lists, own, halo, halo_density, smooth, mass, energy, first, kept, part, volume, wide[:6]
    )
    halo_near, *more = near_halo_call(lists, near, span)
    pull, *_ = force_call(lists, own, halo_near, wide[:3], more)
    packed = pack_call(place.reshape(-1), rows, first, coef, pull, owners)
    migrated, step = migrate_call(packed, least)
    return (migrated, step.reshape(()))


def solution(mesh):
    both = ("slab", "ranges")
    return jax.shard_map(
        per_device,
        mesh=mesh,
        in_specs=(P(None, both), P(both), P(both), P(both, None), P(both)),
        out_specs=(P(None, both), P()),
        check_vma=False,
    )
```

```python
import functools

import jax
import jax.numpy as jnp
from jax import lax
from jax.experimental import pallas as pl
from jax.experimental.pallas import tpu as pltpu
from jax.sharding import PartitionSpec as P

KEY_SPAN = 2048
GAMMA = 5.0 / 3.0
COURANT = 0.3
SMOOTH_ETA = 1.2
REGULAR = 0.02

LANES = 128
SUB = 8
TILES = 4
TERMS = 7
FIRST = (0, 1, 2, 3, 4, 5, 7)
MAIN = 128
REST = 32
TINY = 1e-30
FAR = 4.0
MESH = pl.DeviceIdType.MESH
VMEM = pl.BlockSpec(memory_space=pltpu.VMEM)
SMEM = pl.BlockSpec(memory_space=pltpu.SMEM)


def params(mebibytes, **more):
    return pltpu.CompilerParams(vmem_limit_bytes=mebibytes * 1024 * 1024, **more)


def curve_neighbours():
    slabs, ranges = lax.axis_size("slab"), lax.axis_size("ranges")
    me = lax.axis_index("slab") * ranges + lax.axis_index("ranges")
    after = lax.rem(me + 1, slabs * ranges)
    before = lax.rem(me + slabs * ranges - 1, slabs * ranges)
    return [(d // ranges, lax.rem(d, ranges)) for d in (before, after)]


def swap_halo(own_ref, lists, packed, landed, send_sem, recv_sem, span):
    before, after = curve_neighbours()
    first = lists.shape[0] - 2 * span
    for i in range(2 * span):
        packed[i] = own_ref[lists[first + i]]
    copies = []
    for side, target in ((0, before), (1, after)):
        copy = pltpu.make_async_remote_copy(
            src_ref=packed.at[pl.ds(side * span, span)],
            dst_ref=landed.at[pl.ds((1 - side) * span, span)],
            send_sem=send_sem.at[side],
            recv_sem=recv_sem.at[side],
            device_id=target,
            device_id_type=MESH,
        )
        copy.start()
        copies.append(copy)
    return copies


def greet(partners):
    barrier = pltpu.get_barrier_semaphore()
    for partner in partners:
        pl.semaphore_signal(barrier, inc=1, device_id=partner, device_id_type=MESH)
    return lambda: pl.semaphore_wait(barrier, len(partners))


def slab_partners():
    slabs = lax.axis_size("slab")
    slab, rank = lax.axis_index("slab"), lax.axis_index("ranges")
    return [(lax.rem(slab + t, slabs), rank) for t in range(1, slabs)]


def slot_rows(owner, owners, place_ref):
    blocks = owner.shape[0]
    row, col = (lax.broadcasted_iota(jnp.int32, (LANES, LANES), n) for n in (0, 1))
    upto = (row <= col).astype(jnp.float32).astype(jnp.bfloat16)
    kind = lax.broadcasted_iota(jnp.int32, (owners, LANES), 0)
    ahead = jnp.zeros((owners, 1), jnp.float32)
    for b in range(blocks):
        mine = owner[b : b + 1, :]
        same = (kind == mine).astype(jnp.float32)
        seen = jnp.dot(same.astype(jnp.bfloat16), upto, preferred_element_type=jnp.float32)
        rank = jnp.sum(same * (seen + ahead), axis=0, keepdims=True).astype(jnp.int32) - 1
        ahead = ahead + seen[:, LANES - 1 :]
        place_ref[b : b + 1, :] = jnp.where(
            rank < MAIN, mine * MAIN + rank, owners * MAIN + mine * REST + rank - MAIN
        )


def first_kernel(
    span,
    owners,
    lists,
    state_ref,
    keys_ref,
    halo_ref,
    rows_ref,
    own_ref,
    min_ref,
    place_ref,
    *refs,
):
    wide, (packed, landed, send_sem, recv_sem, least, inbox, put_sem, got_sem) = refs[:TERMS], refs[TERMS:]
    partners = slab_partners()
    wait = greet(curve_neighbours() + partners)
    blocks = own_ref.shape[0]

    def block(b):
        return state_ref[0:SUB, pl.ds(pl.multiple_of(b * LANES, LANES), LANES)]

    for b in range(blocks):
        for f in range(rows_ref.shape[0]):
            rows_ref[f, b : b + 1, :] = state_ref[f : f + 1, b * LANES : (b + 1) * LANES]
    total = rows_ref[3] * rows_ref[3] + rows_ref[4] * rows_ref[4] + rows_ref[5] * rows_ref[5]
    sound = jnp.sqrt(GAMMA * (GAMMA - 1.0) * rows_ref[8])
    least[...] = jnp.full((SUB, LANES), jnp.min(rows_ref[6] / (sound + jnp.sqrt(total))), jnp.float32)
    for b in range(blocks):
        own_ref[b] = block(b)
    wait()
    copies = swap_halo(own_ref, lists, packed, landed, send_sem, recv_sem, span)
    small = []
    for slot, partner in enumerate(partners):
        copy = pltpu.make_async_remote_copy(
            src_ref=least,
            dst_ref=inbox.at[slot],
            send_sem=put_sem.at[slot],
            recv_sem=got_sem.at[slot],
            device_id=partner,
            device_id_type=MESH,
        )
        copy.start()
        small.append(copy)
    spread_all(block, blocks, 0, tuple(zip(wide, FIRST)))
    slot_rows(lax.rem(keys_ref[...] // KEY_SPAN, owners), owners, place_ref)
    for copy in copies:
        copy.wait()
    halo_ref[...] = landed[...]
    value = least[...]
    for slot, copy in enumerate(small):
        copy.wait()
        value = jnp.minimum(value, inbox[slot])
    min_ref[0] = value[0:1]


def first_call(lists, state, keys, span, owners):
    blocks = keys.shape[0]
    slabs = lax.axis_size("slab")
    shape = (2 * span, SUB, LANES)
    space = (blocks + 2 * span) * LANES
    return pl.pallas_call(
        functools.partial(first_kernel, span, owners),
        out_shape=(
            jax.ShapeDtypeStruct(shape, jnp.float32),
            jax.ShapeDtypeStruct((state.shape[0], blocks, LANES), jnp.float32),
            jax.ShapeDtypeStruct((blocks, SUB, LANES), jnp.float32),
            jax.ShapeDtypeStruct((1, 1, LANES), jnp.float32),
            jax.ShapeDtypeStruct((blocks, LANES), jnp.int32),
        )
        + (jax.ShapeDtypeStruct((space, LANES), jnp.float32),) * TERMS,
        in_specs=[SMEM, VMEM, VMEM],
        out_specs=(VMEM,) * (5 + TERMS),
        scratch_shapes=[
            pltpu.VMEM(shape, jnp.float32),
            pltpu.VMEM(shape, jnp.float32),
            pltpu.SemaphoreType.DMA((2,)),
            pltpu.SemaphoreType.DMA((2,)),
            pltpu.VMEM((SUB, LANES), jnp.float32),
            pltpu.VMEM((slabs - 1, SUB, LANES), jnp.float32),
            pltpu.SemaphoreType.DMA((slabs - 1,)),
            pltpu.SemaphoreType.DMA((slabs - 1,)),
        ],
        compiler_params=params(4, collective_id=1, has_side_effects=True),
    )(lists, state, keys)


def density_halo_kernel(span, lists, first_ref, own_ref, kept_ref, *refs):
    wide, (halo_ref, volume_ref, part_ref, packed, landed, send_sem, recv_sem, density) = refs[:6], refs[6:]
    wait = greet(curve_neighbours())
    blocks = own_ref.shape[0]
    for b in range(blocks):
        density[b] = first_ref[0, b : b + 1, :]
    wait()
    copies = swap_halo(density, lists, packed, landed, send_sem, recv_sem, span)
    spread_all(lambda b: with_volume(own_ref[b], density[b]), blocks, 0, ((volume_ref, 7),))
    prepare, load, pair = gradient_parts(own_ref, kept_ref, (*wide, volume_ref))

    def block(b, carry):
        sums = (jnp.zeros((SUB, LANES), jnp.float32),) * part_ref.shape[0]
        sums = one_tile(b * LANES, b * TILES * LANES, load, prepare(b), pair, sums)
        for f, value in enumerate(sums):
            part_ref[f, b] = value
        return carry

    lax.fori_loop(0, blocks, block, 0)
    for copy in copies:
        copy.wait()
    halo_ref[...] = landed[...]


def density_halo_call(lists, first, own, span, kept, wide):
    blocks = own.shape[0]
    shape = (2 * span, 1, LANES)
    return pl.pallas_call(
        functools.partial(density_halo_kernel, span),
        out_shape=(
            jax.ShapeDtypeStruct(shape, jnp.float32),
            jax.ShapeDtypeStruct(((blocks + 2 * span) * LANES, LANES), jnp.float32),
            jax.ShapeDtypeStruct((13, blocks, SUB, LANES), jnp.float32),
        ),
        in_specs=[SMEM] + [VMEM] * 9,
        out_specs=(VMEM, VMEM, VMEM),
        scratch_shapes=[
            pltpu.VMEM(shape, jnp.float32),
            pltpu.VMEM(shape, jnp.float32),
            pltpu.SemaphoreType.DMA((2,)),
            pltpu.SemaphoreType.DMA((2,)),
            pltpu.VMEM((blocks, 1, LANES), jnp.float32),
        ],
        compiler_params=params(4, collective_id=2, has_side_effects=True),
    )(lists, first, own, kept, *wide)


def near_halo_kernel(span, lists, near_ref, halo_ref, *refs):
    greet(curve_neighbours())()
    more, (packed, landed, send_sem, recv_sem) = refs[:TERMS], refs[TERMS:]
    copies = swap_halo(near_ref, lists, packed, landed, send_sem, recv_sem, span)
    spread_all(lambda b: near_ref[b], near_ref.shape[0], 0, tuple((ref, n) for n, ref in enumerate(more)))
    for copy in copies:
        copy.wait()
    halo_ref[...] = landed[...]


def near_halo_call(lists, near, span):
    blocks = near.shape[0]
    shape = (2 * span, SUB, LANES)
    return pl.pallas_call(
        functools.partial(near_halo_kernel, span),
        out_shape=(jax.ShapeDtypeStruct(shape, jnp.float32),)
        + (jax.ShapeDtypeStruct(((blocks + 2 * span) * LANES, LANES), jnp.float32),) * TERMS,
        in_specs=[SMEM, VMEM],
        out_specs=(VMEM,) * (1 + TERMS),
        scratch_shapes=[
            pltpu.VMEM(shape, jnp.float32),
            pltpu.VMEM(shape, jnp.float32),
            pltpu.SemaphoreType.DMA((2,)),
            pltpu.SemaphoreType.DMA((2,)),
        ],
        compiler_params=params(4, collective_id=3, has_side_effects=True),
    )(lists, near)


def spread(rows, start, targets):
    x = jnp.concatenate(rows, axis=1)
    high = x.astype(jnp.bfloat16).astype(jnp.float32)
    middle = (x - high).astype(jnp.bfloat16).astype(jnp.float32)
    parts = jnp.concatenate([high, middle, x - high - middle], axis=0).astype(jnp.bfloat16)
    kind = lax.rem(lax.broadcasted_iota(jnp.int32, (3 * SUB, LANES), 0), SUB)
    at = pl.ds(pl.multiple_of(start * LANES, LANES), x.shape[1])
    for i in range(0, len(targets), 2):
        pair = targets[i : i + 2]
        pick = jnp.concatenate([(kind == f).astype(jnp.float32).astype(jnp.bfloat16) for _, f in pair], axis=1)
        out = lax.dot_general(parts, pick, (((0,), (0,)), ((), ())), preferred_element_type=jnp.float32)
        for m, (ref, _) in enumerate(pair):
            ref[at, :] = out[:, m * LANES : (m + 1) * LANES]


def spread_all(make, count, first, targets, group=10):
    def turn(g, carry):
        spread([make(g * group + i) for i in range(group)], first + g * group, targets)
        return carry

    lax.fori_loop(0, count // group, turn, 0)


def profile(square):
    near = jnp.minimum(square, FAR)
    ratio = near * lax.rsqrt(jnp.maximum(near, TINY))
    outer = jnp.maximum(2.0 - ratio, 0.0)
    inner = jnp.maximum(outer - 1.0, 0.0)
    return outer * outer * (0.25 * outer) - inner * inner * inner


def full(row):
    return jnp.broadcast_to(row, (SUB, LANES))


def shear(w, u):
    return (
        u[0] * w[0],
        u[0] * w[1] + u[1] * w[0],
        u[0] * w[2] + u[2] * w[0],
        u[1] * w[1],
        u[1] * w[2] + u[2] * w[1],
        u[2] * w[2],
    )


def one_tile(start, kept, load, here, pair, sums):
    for s in range(LANES // SUB):
        at = pl.ds(pl.multiple_of(start + s * SUB, SUB), SUB)
        sums = pair(load(at), here, sums, pl.ds(pl.multiple_of(kept + s * SUB, SUB), SUB))
    return sums


def sweep(lists, blocks, width, load, prepare, pair, sums_ref, part_ref=None):
    def block(b, carry):
        here = prepare(b)

        def tile(k, sums):
            return one_tile(lists[b * TILES + k] * LANES, (b * TILES + k) * LANES, load, here, pair, sums)

        if part_ref is None:
            first, sums = 0, (jnp.zeros((SUB, LANES), jnp.float32),) * width
        else:
            first, sums = 1, tuple(part_ref[f, b] for f in range(width))
        sums = lax.fori_loop(first, lists[TILES * blocks + b], tile, sums)
        for f in range(width):
            sums_ref[f, pl.ds(b, 1), :] = jnp.sum(sums[f], axis=0, keepdims=True)
        return carry

    lax.fori_loop(0, blocks, block, 0)


def add(sums, terms):
    return tuple(s + t for s, t in zip(sums, terms))


def density_kernel(lists, own_ref, halo_ref, smooth_ref, *refs):
    out_ref, kept_ref, *wide = refs[TERMS:]
    blocks, halos = own_ref.shape[0], halo_ref.shape[0]
    spread_all(lambda b: halo_ref[b], halos, blocks, tuple(zip(wide, FIRST)))

    def prepare(b):
        h = own_ref[b, 6:7, :]
        return [full(own_ref[b, f : f + 1, :]) for f in range(6)] + [full(1.0 / (h * h))]

    def load(at):
        return [ref[at, :] for ref in wide]

    def pair(c, here, sums, kept):
        d = [c[a] - here[a] for a in range(3)]
        square = d[0] * d[0] + d[1] * d[1] + d[2] * d[2]
        w = profile(square * here[6])
        kept_ref[kept, :] = w
        w = w * c[6]
        wd = [w * d[a] for a in range(3)]
        u = [c[3 + a] - here[3 + a] for a in range(3)]
        return add(sums, (w, *wd, *shear(wd, u)))

    sweep(lists, blocks, 10, load, prepare, pair, out_ref)
    h = smooth_ref[6]
    norm = 1.0 / (jnp.pi * h * h * h)
    for f in range(10):
        out_ref[f] = out_ref[f] * norm


def density_call(lists, own, halo, smooth, wide):
    blocks = own.shape[0]
    return pl.pallas_call(
        density_kernel,
        out_shape=(
            jax.ShapeDtypeStruct((10, blocks, LANES), jnp.float32),
            jax.ShapeDtypeStruct((TILES * blocks * LANES, LANES), jnp.float32),
        )
        + tuple(jax.ShapeDtypeStruct(part.shape, jnp.float32) for part in wide),
        in_specs=[SMEM] + [VMEM] * (3 + TERMS),
        out_specs=(VMEM,) * (2 + TERMS),
        input_output_aliases={4 + n: 2 + n for n in range(TERMS)},
        compiler_params=params(4),
    )(lists, own, halo, smooth, *wide)


def with_volume(rows, density):
    return jnp.concatenate([rows[0:7], rows[7:8] / density], axis=0)


def gradient_parts(own_ref, kept_ref, columns):
    def prepare(b):
        return [full(own_ref[b, f : f + 1, :]) for f in range(6)]

    def load(at):
        return [ref[at, :] for ref in columns]

    def pair(c, here, sums, kept):
        w = kept_ref[kept, :] * c[6]
        d = [c[a] - here[a] for a in range(3)]
        wd = [w * d[a] for a in range(3)]
        u = [c[3 + a] - here[3 + a] for a in range(3)]
        tau = (wd[0] * d[0], wd[0] * d[1], wd[0] * d[2], wd[1] * d[1], wd[1] * d[2], wd[2] * d[2])
        return add(sums, (w, *tau, *shear(wd, u)))

    return prepare, load, pair


def gradient_kernel(
    lists,
    own_ref,
    halo_ref,
    halo_density_ref,
    smooth_ref,
    mass_ref,
    energy_ref,
    first_ref,
    kept_ref,
    part_ref,
    volume_in,
    *refs,
):
    wide, (coef_ref, near_ref, volume_ref, sums_ref) = refs[:6], refs[6:]
    blocks = own_ref.shape[0]

    spread_all(
        lambda b: with_volume(halo_ref[b], halo_density_ref[b]), halo_ref.shape[0], blocks, ((volume_ref, 7),)
    )

    prepare, load, pair = gradient_parts(own_ref, kept_ref, (*wide, volume_ref))
    sweep(lists, blocks, 13, load, prepare, pair, sums_ref, part_ref)
    h = smooth_ref[6]
    norm = 1.0 / (jnp.pi * h * h * h)
    s = [sums_ref[f] * norm for f in range(13)]
    diagonal = REGULAR * h * h * s[0]
    xx, xy, xz, yy, yz, zz = s[1] + diagonal, s[2], s[3], s[4] + diagonal, s[5], s[6] + diagonal
    cof = (
        yy * zz - yz * yz,
        xz * yz - xy * zz,
        xy * yz - xz * yy,
        xx * zz - xz * xz,
        xy * xz - xx * yz,
        xx * yy - xy * xy,
    )
    determinant = xx * cof[0] + xy * cof[1] + xz * cof[2]
    coef = [c / determinant for c in cof]
    divergence = sum(c * t for c, t in zip(coef, s[7:13]))
    density = first_ref[0]
    factor = (GAMMA - 1.0) * density * energy_ref[8] / (density * density)
    heating = -factor * sum(coef[n] * first_ref[4 + n] for n in range(6))
    pull = [first_ref[1 + a] for a in range(3)]
    own_part = [
        factor * (coef[0] * pull[0] + coef[1] * pull[1] + coef[2] * pull[2]),
        factor * (coef[1] * pull[0] + coef[3] * pull[1] + coef[4] * pull[2]),
        factor * (coef[2] * pull[0] + coef[4] * pull[1] + coef[5] * pull[2]),
    ]
    for n, value in enumerate([*coef, divergence, *own_part, heating]):
        coef_ref[n] = value
    scale = mass_ref[7] * factor * norm
    inverse = 1.0 / (h * h)
    for n in range(6):
        sums_ref[n] = coef[n] * scale
    sums_ref[6] = inverse
    sums_ref[7] = inverse

    def regroup(b, carry):
        near_ref[b] = jnp.concatenate([sums_ref[n, pl.ds(b, 1), :] for n in range(8)], axis=0)
        return carry

    lax.fori_loop(0, blocks, regroup, 0)


def gradient_call(lists, own, halo, halo_density, smooth, mass, energy, first, kept, part, volume, wide):
    blocks = own.shape[0]
    return pl.pallas_call(
        gradient_kernel,
        out_shape=(
            jax.ShapeDtypeStruct((11, blocks, LANES), jnp.float32),
            jax.ShapeDtypeStruct((blocks, SUB, LANES), jnp.float32),
            jax.ShapeDtypeStruct(volume.shape, jnp.float32),
        ),
        in_specs=[SMEM] + [VMEM] * 16,
        out_specs=(VMEM,) * 3,
        input_output_aliases={10: 2},
        scratch_shapes=[pltpu.VMEM((13, blocks, LANES), jnp.float32)],
        compiler_params=params(4),
    )(lists, own, halo, halo_density, smooth, mass, energy, first, kept, part, volume, *wide)


def force_kernel(lists, own_ref, halo_near_ref, *refs):
    wide, (out_ref, *more) = refs[:3], refs[3 + TERMS :]
    blocks, halos = own_ref.shape[0], halo_near_ref.shape[0]
    spread_all(lambda b: halo_near_ref[b], halos, blocks, tuple((ref, n) for n, ref in enumerate(more)))

    def prepare(b):
        return [full(own_ref[b, f : f + 1, :]) for f in range(3)]

    def load(at):
        return [ref[at, :] for ref in (*wide, *more)]

    def pair(c, here, sums, kept):
        d = [c[a] - here[a] for a in range(3)]
        square = d[0] * d[0] + d[1] * d[1] + d[2] * d[2]
        w = profile(square * c[9])
        x, y, z = (w * d[a] for a in range(3))
        return (
            sums[0] + c[3] * x + c[4] * y + c[5] * z,
            sums[1] + c[4] * x + c[6] * y + c[7] * z,
            sums[2] + c[5] * x + c[7] * y + c[8] * z,
        )

    sweep(lists, blocks, 3, load, prepare, pair, out_ref)


def force_call(lists, own, halo_near, wide, more):
    blocks = own.shape[0]
    return pl.pallas_call(
        force_kernel,
        out_shape=(jax.ShapeDtypeStruct((3, blocks, LANES), jnp.float32),)
        + tuple(jax.ShapeDtypeStruct(part.shape, jnp.float32) for part in more),
        in_specs=[SMEM] + [VMEM] * (5 + TERMS),
        out_specs=(VMEM,) * (1 + TERMS),
        input_output_aliases={6 + n: 1 + n for n in range(TERMS)},
        compiler_params=params(4),
    )(lists, own, halo_near, *wide, *more)


SENT = 20
PIECE = 5
ROWS = SENT + PIECE


def pack_kernel(place_ref, state_ref, first_ref, coef_ref, pull_ref, out_ref, slots_ref, rows_ref, fields_ref):
    values = [state_ref[f] for f in range(6)] + [first_ref[0], state_ref[7], coef_ref[4], coef_ref[5]]
    values = values + [-(coef_ref[7 + a] + pull_ref[a]) for a in range(3)] + [coef_ref[10], state_ref[8], coef_ref[6]]
    values = values + [coef_ref[n] for n in range(4)]
    for f, value in enumerate(values):
        fields_ref[f] = value
    for f in range(SENT, fields_ref.shape[0]):
        fields_ref[f] = jnp.zeros(fields_ref.shape[1:], jnp.float32)
    count, blocks = fields_ref.shape[0], fields_ref.shape[1]
    owners = out_ref.shape[0]
    span = 3 * count

    def clear(i, carry):
        slots_ref[pl.ds(pl.multiple_of(i * 128, 128), 128), :] = jnp.zeros((128, LANES), jnp.float32)
        return carry

    lax.fori_loop(0, slots_ref.shape[0] // 128, clear, 0)
    row, col = (lax.broadcasted_iota(jnp.int32, (span, LANES), n) for n in (0, 1))
    same = (row == col).astype(jnp.float32).astype(jnp.bfloat16)
    group = 8

    def turn(g, carry):
        rows = [
            jnp.concatenate([fields_ref[f, pl.ds(g * group + i, 1), :] for f in range(count)], axis=0) for i in range(group)
        ]
        x = jnp.concatenate(rows, axis=1)
        high = x.astype(jnp.bfloat16).astype(jnp.float32)
        middle = (x - high).astype(jnp.bfloat16).astype(jnp.float32)
        parts = jnp.concatenate([high, middle, x - high - middle], axis=0).astype(jnp.bfloat16)
        at = pl.ds(pl.multiple_of(g * group * LANES, group * LANES), group * LANES)
        rows_ref[at, :] = lax.dot_general(parts, same, (((0,), (0,)), ((), ())), preferred_element_type=jnp.float32)
        return carry

    lax.fori_loop(0, blocks // group, turn, 0)

    def scatter(b, carry):
        start = pl.multiple_of(b * LANES, LANES)
        for i in range(LANES):
            slots_ref[pl.ds(place_ref[b * LANES + i], 1), :] = rows_ref[pl.ds(start + i, 1), :]
        return carry

    lax.fori_loop(0, blocks, scatter, 0)
    row, col = (lax.broadcasted_iota(jnp.int32, (count, LANES), n) for n in (0, 1))
    gather = ((lax.rem(col, count) == row) & (col < span)).astype(jnp.float32).astype(jnp.bfloat16)

    def turned(at, length):
        rows = slots_ref[pl.ds(at, length), :].astype(jnp.bfloat16)
        return lax.dot_general(gather, rows, (((1,), (1,)), ((), ())), preferred_element_type=jnp.float32)

    def main(g, carry):
        out = turned(pl.multiple_of(g * group * MAIN, MAIN), group * MAIN)
        for i in range(group):
            piece = out[:, i * LANES : (i + 1) * LANES]
            out_ref[g * group + i, 0:SENT, :] = piece[0:SENT]
        return carry

    lax.fori_loop(0, owners // group, main, 0)
    lane = lax.broadcasted_iota(jnp.int32, (PIECE, LANES), 1) // REST

    quarters = LANES // REST
    batch = group * LANES

    def rest(g, carry):
        out = turned(pl.multiple_of(owners * MAIN + g * batch, batch), batch)
        for j in range(group):
            part = out[:, j * LANES : (j + 1) * LANES]
            for i in range(quarters):
                mixed = jnp.zeros((PIECE, LANES), jnp.float32)
                for v in range(SENT // PIECE):
                    piece = part[v * PIECE : (v + 1) * PIECE, :]
                    shift = (v - i) * REST % LANES
                    if shift:
                        piece = pltpu.roll(piece, shift, 1)
                    mixed = jnp.where(lane == v, piece, mixed)
                out_ref[(g * group + j) * quarters + i, SENT:ROWS, :] = mixed
        return carry

    lax.fori_loop(0, owners * REST // batch, rest, 0)


def pack_call(place, state, first, coef, pull, owners):
    blocks = state.shape[1]
    return pl.pallas_call(
        pack_kernel,
        out_shape=jax.ShapeDtypeStruct((owners, ROWS, LANES), jnp.float32),
        in_specs=[SMEM] + [VMEM] * 4,
        out_specs=VMEM,
        scratch_shapes=[
            pltpu.VMEM((owners * (MAIN + REST), LANES), jnp.float32),
            pltpu.VMEM((blocks * LANES, LANES), jnp.float32),
            pltpu.VMEM((24, blocks, LANES), jnp.float32),
        ],
        compiler_params=params(12),
    )(place, state, first, coef, pull)


def cube_root(value):
    size = jnp.abs(value)
    some = size > 0.0
    safe = jnp.where(some, size, 1.0)
    root = jnp.exp(jnp.log(safe) * (1.0 / 3.0))
    root = root - (root - safe / (root * root)) * (1.0 / 3.0)
    return jnp.where(some, jnp.where(value < 0.0, -root, root), 0.0)


def migrate_kernel(in_ref, least_ref, out_ref, step_ref, inbox, minima, send_sem, recv_sem, put_sem, got_sem):
    sources = in_ref.shape[0]
    slab, rank = lax.axis_index("slab"), lax.axis_index("ranges")
    barrier = pltpu.get_barrier_semaphore()

    def hello(t, carry):
        pl.semaphore_signal(barrier, inc=1, device_id=(slab, lax.rem(rank + t, sources)), device_id_type=MESH)
        return carry

    lax.fori_loop(1, sources, hello, 0)
    pl.semaphore_wait(barrier, sources - 1)

    def copy(t):
        to = lax.rem(rank + t, sources)
        return pltpu.make_async_remote_copy(
            src_ref=in_ref.at[to],
            dst_ref=inbox.at[rank],
            send_sem=send_sem.at[t],
            recv_sem=recv_sem.at[rank],
            device_id=(slab, to),
            device_id_type=MESH,
        )

    def tell(t):
        to = lax.rem(rank + t, sources)
        return pltpu.make_async_remote_copy(
            src_ref=least_ref.at[0],
            dst_ref=minima.at[rank],
            send_sem=put_sem.at[t],
            recv_sem=got_sem.at[rank],
            device_id=(slab, to),
            device_id_type=MESH,
        )

    def send(t, carry):
        copy(t).start()
        return carry

    def send_least(t, carry):
        tell(t).start()
        return carry

    lax.fori_loop(1, 8, send, 0)
    lax.fori_loop(1, sources, send_least, 0)
    lax.fori_loop(8, sources, send, 0)
    pltpu.make_async_copy(in_ref.at[rank], inbox.at[rank], recv_sem.at[rank]).start()
    pltpu.make_async_copy(least_ref.at[0], minima.at[rank], got_sem.at[rank]).start()

    def hear(q, carry):
        pltpu.make_async_copy(least_ref.at[0], minima.at[q], got_sem.at[q]).wait()
        return carry

    lax.fori_loop(0, sources, hear, 0)
    step = COURANT * jnp.min(minima[...])
    step_ref[0] = step

    def told(t, carry):
        tell(t).wait_send()
        return carry

    lax.fori_loop(1, sources, told, 0)
    lane = lax.broadcasted_iota(jnp.int32, (SUB, LANES), 1)
    slots = MAIN + REST

    def lay(n, carry):
        g = lax.rem(rank // 4 + sources // 4 - 1 - n, sources // 4)
        for i in range(4):
            q = g * 4 + i
            pltpu.make_async_copy(in_ref.at[q], inbox.at[q], recv_sem.at[q]).wait()
        made = [[None] * 5 for v in range(3)]
        for i in range(4):
            q = g * 4 + i
            c, off = i * slots // LANES, i * slots % LANES
            pieces = []
            last = inbox[q, SENT:ROWS, :]
            for v in range(SENT // PIECE):
                shift = (off - v * REST) % LANES
                pieces.append(pltpu.roll(last, shift, 1) if shift else last)
            rest = jnp.concatenate(pieces, axis=0)
            for v, at in enumerate((0, 8, 16)):
                high = min(at + SUB, SENT)
                columns = made[v]
                place = lane[0 : high - at]
                first = inbox[q, at:high, :]
                moved = pltpu.roll(first, off, 1) if off else first
                columns[c] = jnp.where(place < off, columns[c], moved) if off else moved
                tail = rest[at:high]
                columns[c + 1] = jnp.where(place < off, moved, tail) if off else tail
        for c in range(5):
            low, top, more = (columns[c] for columns in made)
            density, mass, energy = low[6:7], low[7:8], top[6:7]
            ratio = jnp.where(density != 0.0, mass / density, 0.0)
            cols = pl.ds(pl.multiple_of(g * 5 * LANES + c * LANES, LANES), LANES)
            speed = low[3:6] + step * top[2:5]
            out_ref[0:3, cols] = low[0:3] + step * speed
            out_ref[3:6, cols] = speed
            out_ref[6:7, cols] = SMOOTH_ETA * cube_root(ratio)
            out_ref[7:8, cols] = mass
            out_ref[8:9, cols] = energy + step * top[5:6]
            out_ref[9:10, cols] = density
            out_ref[10:11, cols] = (GAMMA - 1.0) * density * energy
            out_ref[11:12, cols] = jnp.sqrt(GAMMA * (GAMMA - 1.0) * energy)
            out_ref[12:16, cols] = more
            out_ref[16:24, cols] = top
        return carry

    lax.fori_loop(0, sources // 4, lay, 0)

    def sent(t, carry):
        copy(t).wait_send()
        return carry

    lax.fori_loop(1, sources, sent, 0)


def migrate_call(packed, least):
    sources = packed.shape[0]
    return pl.pallas_call(
        migrate_kernel,
        out_shape=(
            jax.ShapeDtypeStruct((24, sources * (MAIN + REST)), jnp.float32),
            jax.ShapeDtypeStruct((1,), jnp.float32),
        ),
        in_specs=[VMEM, VMEM],
        out_specs=(VMEM, SMEM),
        scratch_shapes=[
            pltpu.VMEM(packed.shape, jnp.float32),
            pltpu.VMEM((sources, 1, LANES), jnp.float32),
            pltpu.SemaphoreType.DMA((sources,)),
            pltpu.SemaphoreType.DMA((sources,)),
            pltpu.SemaphoreType.DMA((sources,)),
            pltpu.SemaphoreType.DMA((sources,)),
        ],
        compiler_params=params(12, collective_id=4, has_side_effects=True),
    )(packed, least)


def per_device(state, keys, halo_list, neighbour_block_table, neighbour_block_count):
    blocks = neighbour_block_table.shape[0]
    owners = lax.axis_size("ranges")
    lists = jnp.concatenate([neighbour_block_table.reshape(-1), neighbour_block_count, halo_list])
    span = halo_list.shape[0] // 2

    halo, rows, own, least, place, *wide = first_call(lists, state, keys.reshape(blocks, LANES), span, owners)
    first, kept, *wide = density_call(lists, own, halo, rows, wide)
    halo_density, volume, part = density_halo_call(lists, first, own, span, kept, wide[:6])
    coef, near, _ = gradient_call(
        lists, own, halo, halo_density, rows, rows, rows, first, kept, part, volume, wide[:6]
    )
    halo_near, *more = near_halo_call(lists, near, span)
    pull, *_ = force_call(lists, own, halo_near, wide[:3], more)
    packed = pack_call(place.reshape(-1), rows, first, coef, pull, owners)
    migrated, step = migrate_call(packed, least)
    return (migrated, step.reshape(()))


def solution(mesh):
    both = ("slab", "ranges")
    return jax.shard_map(
        per_device,
        mesh=mesh,
        in_specs=(P(None, both), P(both), P(both), P(both, None), P(both)),
        out_specs=(P(None, both), P()),
        check_vma=False,
    )
```

```python
import functools

import jax
import jax.numpy as jnp
from jax import lax
from jax.experimental import pallas as pl
from jax.experimental.pallas import tpu as pltpu
from jax.sharding import PartitionSpec as P

KEY_SPAN = 2048
GAMMA = 5.0 / 3.0
COURANT = 0.3
SMOOTH_ETA = 1.2
REGULAR = 0.02

LANES = 128
SUB = 8
TILES = 4
TERMS = 7
FIRST = (0, 1, 2, 3, 4, 5, 7)
MAIN = 128
REST = 32
TINY = 1e-30
FAR = 4.0
MESH = pl.DeviceIdType.MESH
VMEM = pl.BlockSpec(memory_space=pltpu.VMEM)
SMEM = pl.BlockSpec(memory_space=pltpu.SMEM)


def params(mebibytes, **more):
    return pltpu.CompilerParams(vmem_limit_bytes=mebibytes * 1024 * 1024, **more)


def curve_neighbours():
    slabs, ranges = lax.axis_size("slab"), lax.axis_size("ranges")
    me = lax.axis_index("slab") * ranges + lax.axis_index("ranges")
    after = lax.rem(me + 1, slabs * ranges)
    before = lax.rem(me + slabs * ranges - 1, slabs * ranges)
    return [(d // ranges, lax.rem(d, ranges)) for d in (before, after)]


def swap_halo(own_ref, lists, packed, landed, send_sem, recv_sem, span):
    before, after = curve_neighbours()
    first = lists.shape[0] - 2 * span
    for i in range(2 * span):
        packed[i] = own_ref[lists[first + i]]
    copies = []
    for side, target in ((0, before), (1, after)):
        copy = pltpu.make_async_remote_copy(
            src_ref=packed.at[pl.ds(side * span, span)],
            dst_ref=landed.at[pl.ds((1 - side) * span, span)],
            send_sem=send_sem.at[side],
            recv_sem=recv_sem.at[side],
            device_id=target,
            device_id_type=MESH,
        )
        copy.start()
        copies.append(copy)
    return copies


def greet(partners):
    barrier = pltpu.get_barrier_semaphore()
    for partner in partners:
        pl.semaphore_signal(barrier, inc=1, device_id=partner, device_id_type=MESH)
    return lambda: pl.semaphore_wait(barrier, len(partners))


def slab_partners():
    slabs = lax.axis_size("slab")
    slab, rank = lax.axis_index("slab"), lax.axis_index("ranges")
    return [(lax.rem(slab + t, slabs), rank) for t in range(1, slabs)]


def slot_rows(owner, owners, place_ref):
    blocks = owner.shape[0]
    row, col = (lax.broadcasted_iota(jnp.int32, (LANES, LANES), n) for n in (0, 1))
    upto = (row <= col).astype(jnp.float32).astype(jnp.bfloat16)
    kind = lax.broadcasted_iota(jnp.int32, (owners, LANES), 0)
    ahead = jnp.zeros((owners, 1), jnp.float32)
    for b in range(blocks):
        mine = owner[b : b + 1, :]
        same = (kind == mine).astype(jnp.float32)
        seen = jnp.dot(same.astype(jnp.bfloat16), upto, preferred_element_type=jnp.float32)
        rank = jnp.sum(same * (seen + ahead), axis=0, keepdims=True).astype(jnp.int32) - 1
        ahead = ahead + seen[:, LANES - 1 :]
        place_ref[b : b + 1, :] = jnp.where(
            rank < MAIN, mine * MAIN + rank, owners * MAIN + mine * REST + rank - MAIN
        )


def first_kernel(
    span,
    owners,
    lists,
    state_ref,
    keys_ref,
    halo_ref,
    rows_ref,
    own_ref,
    min_ref,
    place_ref,
    *refs,
):
    wide, (packed, landed, send_sem, recv_sem, least, inbox, put_sem, got_sem) = refs[:TERMS], refs[TERMS:]
    partners = slab_partners()
    wait = greet(curve_neighbours() + partners)
    blocks = own_ref.shape[0]

    def block(b):
        return state_ref[0:SUB, pl.ds(pl.multiple_of(b * LANES, LANES), LANES)]

    for b in range(blocks):
        for f in range(rows_ref.shape[0]):
            rows_ref[f, b : b + 1, :] = state_ref[f : f + 1, b * LANES : (b + 1) * LANES]
    total = rows_ref[3] * rows_ref[3] + rows_ref[4] * rows_ref[4] + rows_ref[5] * rows_ref[5]
    sound = jnp.sqrt(GAMMA * (GAMMA - 1.0) * rows_ref[8])
    least[...] = jnp.full((SUB, LANES), jnp.min(rows_ref[6] / (sound + jnp.sqrt(total))), jnp.float32)
    for b in range(blocks):
        own_ref[b] = block(b)
    wait()
    copies = swap_halo(own_ref, lists, packed, landed, send_sem, recv_sem, span)
    small = []
    for slot, partner in enumerate(partners):
        copy = pltpu.make_async_remote_copy(
            src_ref=least,
            dst_ref=inbox.at[slot],
            send_sem=put_sem.at[slot],
            recv_sem=got_sem.at[slot],
            device_id=partner,
            device_id_type=MESH,
        )
        copy.start()
        small.append(copy)
    spread_all(block, blocks, 0, tuple(zip(wide, FIRST)))
    slot_rows(lax.rem(keys_ref[...] // KEY_SPAN, owners), owners, place_ref)
    for copy in copies:
        copy.wait()
    halo_ref[...] = landed[...]
    value = least[...]
    for slot, copy in enumerate(small):
        copy.wait()
        value = jnp.minimum(value, inbox[slot])
    min_ref[0] = value[0:1]


def first_call(lists, state, keys, span, owners):
    blocks = keys.shape[0]
    slabs = lax.axis_size("slab")
    shape = (2 * span, SUB, LANES)
    space = (blocks + 2 * span) * LANES
    return pl.pallas_call(
        functools.partial(first_kernel, span, owners),
        out_shape=(
            jax.ShapeDtypeStruct(shape, jnp.float32),
            jax.ShapeDtypeStruct((state.shape[0], blocks, LANES), jnp.float32),
            jax.ShapeDtypeStruct((blocks, SUB, LANES), jnp.float32),
            jax.ShapeDtypeStruct((1, 1, LANES), jnp.float32),
            jax.ShapeDtypeStruct((blocks, LANES), jnp.int32),
        )
        + (jax.ShapeDtypeStruct((space, LANES), jnp.float32),) * TERMS,
        in_specs=[SMEM, VMEM, VMEM],
        out_specs=(VMEM,) * (5 + TERMS),
        scratch_shapes=[
            pltpu.VMEM(shape, jnp.float32),
            pltpu.VMEM(shape, jnp.float32),
            pltpu.SemaphoreType.DMA((2,)),
            pltpu.SemaphoreType.DMA((2,)),
            pltpu.VMEM((SUB, LANES), jnp.float32),
            pltpu.VMEM((slabs - 1, SUB, LANES), jnp.float32),
            pltpu.SemaphoreType.DMA((slabs - 1,)),
            pltpu.SemaphoreType.DMA((slabs - 1,)),
        ],
        compiler_params=params(4, collective_id=1, has_side_effects=True),
    )(lists, state, keys)


def density_halo_kernel(span, lists, first_ref, own_ref, kept_ref, *refs):
    wide, (halo_ref, volume_ref, part_ref, packed, landed, send_sem, recv_sem, density) = refs[:6], refs[6:]
    wait = greet(curve_neighbours())
    blocks = own_ref.shape[0]
    for b in range(blocks):
        density[b] = first_ref[0, b : b + 1, :]
    wait()
    copies = swap_halo(density, lists, packed, landed, send_sem, recv_sem, span)
    spread_all(lambda b: with_volume(own_ref[b], density[b]), blocks, 0, ((volume_ref, 7),))
    prepare, load, pair = gradient_parts(own_ref, kept_ref, (*wide, volume_ref))

    def block(b, carry):
        sums = (jnp.zeros((SUB, LANES), jnp.float32),) * part_ref.shape[0]
        sums = one_tile(b * LANES, b * TILES * LANES, load, prepare(b), pair, sums)
        for f, value in enumerate(sums):
            part_ref[f, b] = value
        return carry

    lax.fori_loop(0, blocks, block, 0)
    for copy in copies:
        copy.wait()
    halo_ref[...] = landed[...]


def density_halo_call(lists, first, own, span, kept, wide):
    blocks = own.shape[0]
    shape = (2 * span, 1, LANES)
    return pl.pallas_call(
        functools.partial(density_halo_kernel, span),
        out_shape=(
            jax.ShapeDtypeStruct(shape, jnp.float32),
            jax.ShapeDtypeStruct(((blocks + 2 * span) * LANES, LANES), jnp.float32),
            jax.ShapeDtypeStruct((13, blocks, SUB, LANES), jnp.float32),
        ),
        in_specs=[SMEM] + [VMEM] * 9,
        out_specs=(VMEM, VMEM, VMEM),
        scratch_shapes=[
            pltpu.VMEM(shape, jnp.float32),
            pltpu.VMEM(shape, jnp.float32),
            pltpu.SemaphoreType.DMA((2,)),
            pltpu.SemaphoreType.DMA((2,)),
            pltpu.VMEM((blocks, 1, LANES), jnp.float32),
        ],
        compiler_params=params(4, collective_id=2, has_side_effects=True),
    )(lists, first, own, kept, *wide)


def near_halo_kernel(span, lists, near_ref, own_ref, x_ref, y_ref, z_ref, halo_ref, part_ref, *refs):
    greet(curve_neighbours())()
    more, (packed, landed, send_sem, recv_sem) = refs[:TERMS], refs[TERMS:]
    copies = swap_halo(near_ref, lists, packed, landed, send_sem, recv_sem, span)
    spread_all(lambda b: near_ref[b], near_ref.shape[0], 0, tuple((ref, n) for n, ref in enumerate(more)))
    prepare, load, pair = force_parts(own_ref, (x_ref, y_ref, z_ref, *more))

    def block(b, carry):
        sums = (jnp.zeros((SUB, LANES), jnp.float32),) * part_ref.shape[0]
        sums = one_tile(b * LANES, b * TILES * LANES, load, prepare(b), pair, sums)
        for f, value in enumerate(sums):
            part_ref[f, b] = value
        return carry

    lax.fori_loop(0, near_ref.shape[0], block, 0)
    for copy in copies:
        copy.wait()
    halo_ref[...] = landed[...]


def near_halo_call(lists, near, span, own, wide):
    blocks = near.shape[0]
    shape = (2 * span, SUB, LANES)
    return pl.pallas_call(
        functools.partial(near_halo_kernel, span),
        out_shape=(
            jax.ShapeDtypeStruct(shape, jnp.float32),
            jax.ShapeDtypeStruct((3, blocks, SUB, LANES), jnp.float32),
        )
        + (jax.ShapeDtypeStruct(((blocks + 2 * span) * LANES, LANES), jnp.float32),) * TERMS,
        in_specs=[SMEM] + [VMEM] * 5,
        out_specs=(VMEM,) * (2 + TERMS),
        scratch_shapes=[
            pltpu.VMEM(shape, jnp.float32),
            pltpu.VMEM(shape, jnp.float32),
            pltpu.SemaphoreType.DMA((2,)),
            pltpu.SemaphoreType.DMA((2,)),
        ],
        compiler_params=params(4, collective_id=3, has_side_effects=True),
    )(lists, near, own, *wide)


def spread(rows, start, targets):
    x = jnp.concatenate(rows, axis=1)
    high = x.astype(jnp.bfloat16).astype(jnp.float32)
    middle = (x - high).astype(jnp.bfloat16).astype(jnp.float32)
    parts = jnp.concatenate([high, middle, x - high - middle], axis=0).astype(jnp.bfloat16)
    kind = lax.rem(lax.broadcasted_iota(jnp.int32, (3 * SUB, LANES), 0), SUB)
    at = pl.ds(pl.multiple_of(start * LANES, LANES), x.shape[1])
    for i in range(0, len(targets), 2):
        pair = targets[i : i + 2]
        pick = jnp.concatenate([(kind == f).astype(jnp.float32).astype(jnp.bfloat16) for _, f in pair], axis=1)
        out = lax.dot_general(parts, pick, (((0,), (0,)), ((), ())), preferred_element_type=jnp.float32)
        for m, (ref, _) in enumerate(pair):
            ref[at, :] = out[:, m * LANES : (m + 1) * LANES]


def spread_all(make, count, first, targets, group=10):
    def turn(g, carry):
        spread([make(g * group + i) for i in range(group)], first + g * group, targets)
        return carry

    lax.fori_loop(0, count // group, turn, 0)


def profile(square):
    near = jnp.minimum(square, FAR)
    ratio = near * lax.rsqrt(jnp.maximum(near, TINY))
    outer = jnp.maximum(2.0 - ratio, 0.0)
    inner = jnp.maximum(outer - 1.0, 0.0)
    return outer * outer * (0.25 * outer) - inner * inner * inner


def full(row):
    return jnp.broadcast_to(row, (SUB, LANES))


def shear(w, u):
    return (
        u[0] * w[0],
        u[0] * w[1] + u[1] * w[0],
        u[0] * w[2] + u[2] * w[0],
        u[1] * w[1],
        u[1] * w[2] + u[2] * w[1],
        u[2] * w[2],
    )


def one_tile(start, kept, load, here, pair, sums):
    for s in range(LANES // SUB):
        at = pl.ds(pl.multiple_of(start + s * SUB, SUB), SUB)
        sums = pair(load(at), here, sums, pl.ds(pl.multiple_of(kept + s * SUB, SUB), SUB))
    return sums


def sweep(lists, blocks, width, load, prepare, pair, sums_ref, part_ref=None):
    def block(b, carry):
        here = prepare(b)

        def tile(k, sums):
            return one_tile(lists[b * TILES + k] * LANES, (b * TILES + k) * LANES, load, here, pair, sums)

        if part_ref is None:
            first, sums = 0, (jnp.zeros((SUB, LANES), jnp.float32),) * width
        else:
            first, sums = 1, tuple(part_ref[f, b] for f in range(width))
        sums = lax.fori_loop(first, lists[TILES * blocks + b], tile, sums)
        for f in range(width):
            sums_ref[f, pl.ds(b, 1), :] = jnp.sum(sums[f], axis=0, keepdims=True)
        return carry

    lax.fori_loop(0, blocks, block, 0)


def add(sums, terms):
    return tuple(s + t for s, t in zip(sums, terms))


def density_kernel(lists, own_ref, halo_ref, smooth_ref, *refs):
    out_ref, kept_ref, *wide = refs[TERMS:]
    blocks, halos = own_ref.shape[0], halo_ref.shape[0]
    spread_all(lambda b: halo_ref[b], halos, blocks, tuple(zip(wide, FIRST)))

    def prepare(b):
        h = own_ref[b, 6:7, :]
        return [full(own_ref[b, f : f + 1, :]) for f in range(6)] + [full(1.0 / (h * h))]

    def load(at):
        return [ref[at, :] for ref in wide]

    def pair(c, here, sums, kept):
        d = [c[a] - here[a] for a in range(3)]
        square = d[0] * d[0] + d[1] * d[1] + d[2] * d[2]
        w = profile(square * here[6])
        kept_ref[kept, :] = w
        w = w * c[6]
        wd = [w * d[a] for a in range(3)]
        u = [c[3 + a] - here[3 + a] for a in range(3)]
        return add(sums, (w, *wd, *shear(wd, u)))

    sweep(lists, blocks, 10, load, prepare, pair, out_ref)
    h = smooth_ref[6]
    norm = 1.0 / (jnp.pi * h * h * h)
    for f in range(10):
        out_ref[f] = out_ref[f] * norm


def density_call(lists, own, halo, smooth, wide):
    blocks = own.shape[0]
    return pl.pallas_call(
        density_kernel,
        out_shape=(
            jax.ShapeDtypeStruct((10, blocks, LANES), jnp.float32),
            jax.ShapeDtypeStruct((TILES * blocks * LANES, LANES), jnp.float32),
        )
        + tuple(jax.ShapeDtypeStruct(part.shape, jnp.float32) for part in wide),
        in_specs=[SMEM] + [VMEM] * (3 + TERMS),
        out_specs=(VMEM,) * (2 + TERMS),
        input_output_aliases={4 + n: 2 + n for n in range(TERMS)},
        compiler_params=params(4),
    )(lists, own, halo, smooth, *wide)


def with_volume(rows, density):
    return jnp.concatenate([rows[0:7], rows[7:8] / density], axis=0)


def gradient_parts(own_ref, kept_ref, columns):
    def prepare(b):
        return [full(own_ref[b, f : f + 1, :]) for f in range(6)]

    def load(at):
        return [ref[at, :] for ref in columns]

    def pair(c, here, sums, kept):
        w = kept_ref[kept, :] * c[6]
        d = [c[a] - here[a] for a in range(3)]
        wd = [w * d[a] for a in range(3)]
        u = [c[3 + a] - here[3 + a] for a in range(3)]
        tau = (wd[0] * d[0], wd[0] * d[1], wd[0] * d[2], wd[1] * d[1], wd[1] * d[2], wd[2] * d[2])
        return add(sums, (w, *tau, *shear(wd, u)))

    return prepare, load, pair


def gradient_kernel(
    lists,
    own_ref,
    halo_ref,
    halo_density_ref,
    smooth_ref,
    mass_ref,
    energy_ref,
    first_ref,
    kept_ref,
    part_ref,
    volume_in,
    *refs,
):
    wide, (coef_ref, near_ref, volume_ref, sums_ref) = refs[:6], refs[6:]
    blocks = own_ref.shape[0]

    spread_all(
        lambda b: with_volume(halo_ref[b], halo_density_ref[b]), halo_ref.shape[0], blocks, ((volume_ref, 7),)
    )

    prepare, load, pair = gradient_parts(own_ref, kept_ref, (*wide, volume_ref))
    sweep(lists, blocks, 13, load, prepare, pair, sums_ref, part_ref)
    h = smooth_ref[6]
    norm = 1.0 / (jnp.pi * h * h * h)
    s = [sums_ref[f] * norm for f in range(13)]
    diagonal = REGULAR * h * h * s[0]
    xx, xy, xz, yy, yz, zz = s[1] + diagonal, s[2], s[3], s[4] + diagonal, s[5], s[6] + diagonal
    cof = (
        yy * zz - yz * yz,
        xz * yz - xy * zz,
        xy * yz - xz * yy,
        xx * zz - xz * xz,
        xy * xz - xx * yz,
        xx * yy - xy * xy,
    )
    determinant = xx * cof[0] + xy * cof[1] + xz * cof[2]
    coef = [c / determinant for c in cof]
    divergence = sum(c * t for c, t in zip(coef, s[7:13]))
    density = first_ref[0]
    factor = (GAMMA - 1.0) * density * energy_ref[8] / (density * density)
    heating = -factor * sum(coef[n] * first_ref[4 + n] for n in range(6))
    pull = [first_ref[1 + a] for a in range(3)]
    own_part = [
        factor * (coef[0] * pull[0] + coef[1] * pull[1] + coef[2] * pull[2]),
        factor * (coef[1] * pull[0] + coef[3] * pull[1] + coef[4] * pull[2]),
        factor * (coef[2] * pull[0] + coef[4] * pull[1] + coef[5] * pull[2]),
    ]
    for n, value in enumerate([*coef, divergence, *own_part, heating]):
        coef_ref[n] = value
    scale = mass_ref[7] * factor * norm
    inverse = 1.0 / (h * h)
    for n in range(6):
        sums_ref[n] = coef[n] * scale
    sums_ref[6] = inverse
    sums_ref[7] = inverse

    def regroup(b, carry):
        near_ref[b] = jnp.concatenate([sums_ref[n, pl.ds(b, 1), :] for n in range(8)], axis=0)
        return carry

    lax.fori_loop(0, blocks, regroup, 0)


def gradient_call(lists, own, halo, halo_density, smooth, mass, energy, first, kept, part, volume, wide):
    blocks = own.shape[0]
    return pl.pallas_call(
        gradient_kernel,
        out_shape=(
            jax.ShapeDtypeStruct((11, blocks, LANES), jnp.float32),
            jax.ShapeDtypeStruct((blocks, SUB, LANES), jnp.float32),
            jax.ShapeDtypeStruct(volume.shape, jnp.float32),
        ),
        in_specs=[SMEM] + [VMEM] * 16,
        out_specs=(VMEM,) * 3,
        input_output_aliases={10: 2},
        scratch_shapes=[pltpu.VMEM((13, blocks, LANES), jnp.float32)],
        compiler_params=params(4),
    )(lists, own, halo, halo_density, smooth, mass, energy, first, kept, part, volume, *wide)


def force_parts(own_ref, columns):
    def prepare(b):
        return [full(own_ref[b, f : f + 1, :]) for f in range(3)]

    def load(at):
        return [ref[at, :] for ref in columns]

    def pair(c, here, sums, kept):
        d = [c[a] - here[a] for a in range(3)]
        square = d[0] * d[0] + d[1] * d[1] + d[2] * d[2]
        w = profile(square * c[9])
        x, y, z = (w * d[a] for a in range(3))
        return (
            sums[0] + c[3] * x + c[4] * y + c[5] * z,
            sums[1] + c[4] * x + c[6] * y + c[7] * z,
            sums[2] + c[5] * x + c[7] * y + c[8] * z,
        )

    return prepare, load, pair


def force_kernel(lists, own_ref, halo_near_ref, part_ref, *refs):
    wide, (out_ref, *more) = refs[:3], refs[3 + TERMS :]
    blocks, halos = own_ref.shape[0], halo_near_ref.shape[0]
    spread_all(lambda b: halo_near_ref[b], halos, blocks, tuple((ref, n) for n, ref in enumerate(more)))

    prepare, load, pair = force_parts(own_ref, (*wide, *more))
    sweep(lists, blocks, 3, load, prepare, pair, out_ref, part_ref)


def force_call(lists, own, halo_near, part, wide, more):
    blocks = own.shape[0]
    return pl.pallas_call(
        force_kernel,
        out_shape=(jax.ShapeDtypeStruct((3, blocks, LANES), jnp.float32),)
        + tuple(jax.ShapeDtypeStruct(part.shape, jnp.float32) for part in more),
        in_specs=[SMEM] + [VMEM] * (6 + TERMS),
        out_specs=(VMEM,) * (1 + TERMS),
        input_output_aliases={7 + n: 1 + n for n in range(TERMS)},
        compiler_params=params(4),
    )(lists, own, halo_near, part, *wide, *more)


SENT = 20
PIECE = 5
ROWS = SENT + PIECE


def pack_kernel(place_ref, state_ref, first_ref, coef_ref, pull_ref, out_ref, slots_ref, rows_ref, fields_ref):
    values = [state_ref[f] for f in range(6)] + [first_ref[0], state_ref[7], coef_ref[4], coef_ref[5]]
    values = values + [-(coef_ref[7 + a] + pull_ref[a]) for a in range(3)] + [coef_ref[10], state_ref[8], coef_ref[6]]
    values = values + [coef_ref[n] for n in range(4)]
    for f, value in enumerate(values):
        fields_ref[f] = value
    for f in range(SENT, fields_ref.shape[0]):
        fields_ref[f] = jnp.zeros(fields_ref.shape[1:], jnp.float32)
    count, blocks = fields_ref.shape[0], fields_ref.shape[1]
    owners = out_ref.shape[0]
    span = 3 * count

    def clear(i, carry):
        slots_ref[pl.ds(pl.multiple_of(i * 128, 128), 128), :] = jnp.zeros((128, LANES), jnp.float32)
        return carry

    lax.fori_loop(0, slots_ref.shape[0] // 128, clear, 0)
    row, col = (lax.broadcasted_iota(jnp.int32, (span, LANES), n) for n in (0, 1))
    same = (row == col).astype(jnp.float32).astype(jnp.bfloat16)
    group = 8

    def turn(g, carry):
        rows = [
            jnp.concatenate([fields_ref[f, pl.ds(g * group + i, 1), :] for f in range(count)], axis=0) for i in range(group)
        ]
        x = jnp.concatenate(rows, axis=1)
        high = x.astype(jnp.bfloat16).astype(jnp.float32)
        middle = (x - high).astype(jnp.bfloat16).astype(jnp.float32)
        parts = jnp.concatenate([high, middle, x - high - middle], axis=0).astype(jnp.bfloat16)
        at = pl.ds(pl.multiple_of(g * group * LANES, group * LANES), group * LANES)
        rows_ref[at, :] = lax.dot_general(parts, same, (((0,), (0,)), ((), ())), preferred_element_type=jnp.float32)
        return carry

    lax.fori_loop(0, blocks // group, turn, 0)

    def scatter(b, carry):
        start = pl.multiple_of(b * LANES, LANES)
        for i in range(LANES):
            slots_ref[pl.ds(place_ref[b * LANES + i], 1), :] = rows_ref[pl.ds(start + i, 1), :]
        return carry

    lax.fori_loop(0, blocks, scatter, 0)
    row, col = (lax.broadcasted_iota(jnp.int32, (count, LANES), n) for n in (0, 1))
    gather = ((lax.rem(col, count) == row) & (col < span)).astype(jnp.float32).astype(jnp.bfloat16)

    def turned(at, length):
        rows = slots_ref[pl.ds(at, length), :].astype(jnp.bfloat16)
        return lax.dot_general(gather, rows, (((1,), (1,)), ((), ())), preferred_element_type=jnp.float32)

    def main(g, carry):
        out = turned(pl.multiple_of(g * group * MAIN, MAIN), group * MAIN)
        for i in range(group):
            piece = out[:, i * LANES : (i + 1) * LANES]
            out_ref[g * group + i, 0:SENT, :] = piece[0:SENT]
        return carry

    lax.fori_loop(0, owners // group, main, 0)
    lane = lax.broadcasted_iota(jnp.int32, (PIECE, LANES), 1) // REST

    quarters = LANES // REST
    batch = group * LANES

    def rest(g, carry):
        out = turned(pl.multiple_of(owners * MAIN + g * batch, batch), batch)
        for j in range(group):
            part = out[:, j * LANES : (j + 1) * LANES]
            for i in range(quarters):
                mixed = jnp.zeros((PIECE, LANES), jnp.float32)
                for v in range(SENT // PIECE):
                    piece = part[v * PIECE : (v + 1) * PIECE, :]
                    shift = (v - i) * REST % LANES
                    if shift:
                        piece = pltpu.roll(piece, shift, 1)
                    mixed = jnp.where(lane == v, piece, mixed)
                out_ref[(g * group + j) * quarters + i, SENT:ROWS, :] = mixed
        return carry

    lax.fori_loop(0, owners * REST // batch, rest, 0)


def pack_call(place, state, first, coef, pull, owners):
    blocks = state.shape[1]
    return pl.pallas_call(
        pack_kernel,
        out_shape=jax.ShapeDtypeStruct((owners, ROWS, LANES), jnp.float32),
        in_specs=[SMEM] + [VMEM] * 4,
        out_specs=VMEM,
        scratch_shapes=[
            pltpu.VMEM((owners * (MAIN + REST), LANES), jnp.float32),
            pltpu.VMEM((blocks * LANES, LANES), jnp.float32),
            pltpu.VMEM((24, blocks, LANES), jnp.float32),
        ],
        compiler_params=params(12),
    )(place, state, first, coef, pull)


def cube_root(value):
    size = jnp.abs(value)
    some = size > 0.0
    safe = jnp.where(some, size, 1.0)
    root = jnp.exp(jnp.log(safe) * (1.0 / 3.0))
    root = root - (root - safe / (root * root)) * (1.0 / 3.0)
    return jnp.where(some, jnp.where(value < 0.0, -root, root), 0.0)


def migrate_kernel(in_ref, least_ref, out_ref, step_ref, inbox, minima, send_sem, recv_sem, put_sem, got_sem):
    sources = in_ref.shape[0]
    slab, rank = lax.axis_index("slab"), lax.axis_index("ranges")
    barrier = pltpu.get_barrier_semaphore()

    def hello(t, carry):
        pl.semaphore_signal(barrier, inc=1, device_id=(slab, lax.rem(rank + t, sources)), device_id_type=MESH)
        return carry

    lax.fori_loop(1, sources, hello, 0)
    pl.semaphore_wait(barrier, sources - 1)

    def copy(t):
        to = lax.rem(rank + t, sources)
        return pltpu.make_async_remote_copy(
            src_ref=in_ref.at[to],
            dst_ref=inbox.at[rank],
            send_sem=send_sem.at[t],
            recv_sem=recv_sem.at[rank],
            device_id=(slab, to),
            device_id_type=MESH,
        )

    def tell(t):
        to = lax.rem(rank + t, sources)
        return pltpu.make_async_remote_copy(
            src_ref=least_ref.at[0],
            dst_ref=minima.at[rank],
            send_sem=put_sem.at[t],
            recv_sem=got_sem.at[rank],
            device_id=(slab, to),
            device_id_type=MESH,
        )

    def send(t, carry):
        copy(t).start()
        return carry

    def send_least(t, carry):
        tell(t).start()
        return carry

    lax.fori_loop(1, 8, send, 0)
    lax.fori_loop(1, sources, send_least, 0)
    lax.fori_loop(8, sources, send, 0)
    pltpu.make_async_copy(in_ref.at[rank], inbox.at[rank], recv_sem.at[rank]).start()
    pltpu.make_async_copy(least_ref.at[0], minima.at[rank], got_sem.at[rank]).start()

    def hear(q, carry):
        pltpu.make_async_copy(least_ref.at[0], minima.at[q], got_sem.at[q]).wait()
        return carry

    lax.fori_loop(0, sources, hear, 0)
    step = COURANT * jnp.min(minima[...])
    step_ref[0] = step

    def told(t, carry):
        tell(t).wait_send()
        return carry

    lax.fori_loop(1, sources, told, 0)
    lane = lax.broadcasted_iota(jnp.int32, (SUB, LANES), 1)
    slots = MAIN + REST

    def lay(n, carry):
        g = lax.rem(rank // 4 + sources // 4 - 1 - n, sources // 4)
        for i in range(4):
            q = g * 4 + i
            pltpu.make_async_copy(in_ref.at[q], inbox.at[q], recv_sem.at[q]).wait()
        made = [[None] * 5 for v in range(3)]
        for i in range(4):
            q = g * 4 + i
            c, off = i * slots // LANES, i * slots % LANES
            pieces = []
            last = inbox[q, SENT:ROWS, :]
            for v in range(SENT // PIECE):
                shift = (off - v * REST) % LANES
                pieces.append(pltpu.roll(last, shift, 1) if shift else last)
            rest = jnp.concatenate(pieces, axis=0)
            for v, at in enumerate((0, 8, 16)):
                high = min(at + SUB, SENT)
                columns = made[v]
                place = lane[0 : high - at]
                first = inbox[q, at:high, :]
                moved = pltpu.roll(first, off, 1) if off else first
                columns[c] = jnp.where(place < off, columns[c], moved) if off else moved
                tail = rest[at:high]
                columns[c + 1] = jnp.where(place < off, moved, tail) if off else tail
        for c in range(5):
            low, top, more = (columns[c] for columns in made)
            density, mass, energy = low[6:7], low[7:8], top[6:7]
            ratio = jnp.where(density != 0.0, mass / density, 0.0)
            cols = pl.ds(pl.multiple_of(g * 5 * LANES + c * LANES, LANES), LANES)
            speed = low[3:6] + step * top[2:5]
            out_ref[0:3, cols] = low[0:3] + step * speed
            out_ref[3:6, cols] = speed
            out_ref[6:7, cols] = SMOOTH_ETA * cube_root(ratio)
            out_ref[7:8, cols] = mass
            out_ref[8:9, cols] = energy + step * top[5:6]
            out_ref[9:10, cols] = density
            out_ref[10:11, cols] = (GAMMA - 1.0) * density * energy
            out_ref[11:12, cols] = jnp.sqrt(GAMMA * (GAMMA - 1.0) * energy)
            out_ref[12:16, cols] = more
            out_ref[16:24, cols] = top
        return carry

    lax.fori_loop(0, sources // 4, lay, 0)

    def sent(t, carry):
        copy(t).wait_send()
        return carry

    lax.fori_loop(1, sources, sent, 0)


def migrate_call(packed, least):
    sources = packed.shape[0]
    return pl.pallas_call(
        migrate_kernel,
        out_shape=(
            jax.ShapeDtypeStruct((24, sources * (MAIN + REST)), jnp.float32),
            jax.ShapeDtypeStruct((1,), jnp.float32),
        ),
        in_specs=[VMEM, VMEM],
        out_specs=(VMEM, SMEM),
        scratch_shapes=[
            pltpu.VMEM(packed.shape, jnp.float32),
            pltpu.VMEM((sources, 1, LANES), jnp.float32),
            pltpu.SemaphoreType.DMA((sources,)),
            pltpu.SemaphoreType.DMA((sources,)),
            pltpu.SemaphoreType.DMA((sources,)),
            pltpu.SemaphoreType.DMA((sources,)),
        ],
        compiler_params=params(12, collective_id=4, has_side_effects=True),
    )(packed, least)


def per_device(state, keys, halo_list, neighbour_block_table, neighbour_block_count):
    blocks = neighbour_block_table.shape[0]
    owners = lax.axis_size("ranges")
    lists = jnp.concatenate([neighbour_block_table.reshape(-1), neighbour_block_count, halo_list])
    span = halo_list.shape[0] // 2

    halo, rows, own, least, place, *wide = first_call(lists, state, keys.reshape(blocks, LANES), span, owners)
    first, kept, *wide = density_call(lists, own, halo, rows, wide)
    halo_density, volume, part = density_halo_call(lists, first, own, span, kept, wide[:6])
    coef, near, _ = gradient_call(
        lists, own, halo, halo_density, rows, rows, rows, first, kept, part, volume, wide[:6]
    )
    halo_near, part, *more = near_halo_call(lists, near, span, own, wide[:3])
    pull, *_ = force_call(lists, own, halo_near, part, wide[:3], more)
    packed = pack_call(place.reshape(-1), rows, first, coef, pull, owners)
    migrated, step = migrate_call(packed, least)
    return (migrated, step.reshape(()))


def solution(mesh):
    both = ("slab", "ranges")
    return jax.shard_map(
        per_device,
        mesh=mesh,
        in_specs=(P(None, both), P(both), P(both), P(both, None), P(both)),
        out_specs=(P(None, both), P()),
        check_vma=False,
    )
```
